512 devices in a mesh: row: 32 (over y, x_lo, core), col: 16 (over x_hi, z).
Axes of the slice: x: 4 (x_hi: 2, x_lo: 2; x = x_hi * 2 + x_lo), y: 8, z: 8, core: 2. Of those that a mesh axis runs over, the one named last changes fastest.
Arguments:
- object_field: float32 [2, 8192, 8192], P(None, 'row', 'col'), may hold values from -6 to 6
- probe_field: float32 [2, 256, 256], replicated, may hold values from -6 to 6
- intensity: float32 [2048, 256, 256], P(('row', 'col')), may hold values from 0.05 to 4
- offsets: int32 [2048, 2], P(('row', 'col')), may hold values from 0 to 8191, as said below
- counts: int32 [512], P(('row', 'col')), may hold values from 1 to 4, as said below
Outputs:
- object_grad: float32 [2, 8192, 8192], P(None, 'row', 'col')
- probe_grad: float32 [2, 256, 256], replicated
The draws below stay inside these ranges and needn't reach their ends.
Inputs may be any that keep to these rules, and one draw needn't show every extreme that they name: `offsets`: slot j belongs to the device j // 4 in row-major order over row and col, and its upper left corner lies in that device's object tile. `counts`: some device has all 4 slots live.
All inputs are finite; a program needn't handle non-finite values.
Results may differ from the reference program's by a relative error of at most 0.0003.
Values sent between devices are 32-bit elements; how exact they have to be, the bound alone decides.
A program may use at most 64 MiB of HBM per device.

```python
import math
import jax
import jax.numpy as jnp
from jax import lax

PATCH = 256
TILE_R = 256
TILE_C = 512
P_DEV = 4
NY = 8192
NX = 8192
POSITIONS = 2048


def draw_offsets(key, part):
    key = jax.random.fold_in(key, 11)
    row_key, col_key = jax.random.split(key)
    slot_ids = jnp.arange(POSITIONS, dtype=jnp.int32)
    device = slot_ids // P_DEV
    tiles_across = NX // TILE_C
    tile_row = device // tiles_across
    tile_col = device % tiles_across
    local_row = jax.random.randint(row_key, (POSITIONS,), 0, TILE_R, dtype=jnp.int32)
    local_col = jax.random.randint(col_key, (POSITIONS,), 0, TILE_C, dtype=jnp.int32)
    local_row = local_row.at[0].set(0).at[POSITIONS - 1].set(TILE_R - 1)
    local_col = local_col.at[0].set(0).at[POSITIONS - 1].set(TILE_C - 1)
    return jnp.stack([tile_row * TILE_R + local_row, tile_col * TILE_C + local_col], axis=1).astype(jnp.int32)


def draw_counts(key, part):
    key = jax.random.fold_in(key, 23)
    count_key, full_key = jax.random.split(key)
    devices_total = NY // TILE_R * (NX // TILE_C)
    values = jax.random.randint(count_key, (devices_total,), 1, P_DEV + 1, dtype=jnp.int32)
    busiest = jax.random.randint(full_key, (), 0, devices_total, dtype=jnp.int32)
    return values.at[busiest].set(P_DEV).astype(jnp.int32)


def block_levels(own_key, dims, pieces, smallest, largest):
    factor_of, own = 1.0, jax.random.fold_in(own_key, 6)
    for position, parts in pieces:
        heights = jnp.exp(jax.random.uniform(jax.random.fold_in(own, position), (parts,), jnp.float32, smallest / len(pieces), largest / len(pieces)))
        factor_of = factor_of * jnp.repeat(heights, dims[position] // parts).reshape([-1 if axis == position else 1 for axis in range(len(dims))])
    return factor_of


def noise(own_key, shape, deviation, reach, cuts=(), kind=jnp.bfloat16):
    values = deviation * jax.random.normal(own_key, shape, jnp.float32)
    if cuts:
        values = values * block_levels(own_key, shape, cuts, -0.22, 0.18)
    return jnp.clip(values, -reach, reach).astype(kind)


def setup_inputs(seed: int = 0) -> dict:
    key_list = jax.random.split(jax.random.key(seed), 6)
    object_field = noise(key_list[0], (2, NY, NX), 1.0, 6.0, ((1, 32), (2, 16)), jnp.float32)
    probe_field = noise(key_list[1], (2, PATCH, PATCH), 1.0, 6.0, (), jnp.float32)
    intensity = jnp.clip(jnp.exp(math.log(4.0) - 4.3820266 * jax.random.uniform(key_list[2], (POSITIONS, PATCH, PATCH), jnp.float32) ** block_levels(key_list[2], (POSITIONS, PATCH, PATCH), ((0, 512),), -0.2, 0.2)), 0.05, 4.0)
    offsets = draw_offsets(jax.random.fold_in(key_list[5], 71), 0)
    counts = draw_counts(jax.random.fold_in(key_list[5], 71), 0)
    return {"object_field": object_field, "probe_field": probe_field, "intensity": intensity, "offsets": offsets, "counts": counts}


stabilizer = 0.01

def reference(object_field, probe_field, intensity, offsets, counts):
    whole = lax.complex(object_field[0], object_field[1])
    padded = jnp.pad(whole, ((0, PATCH), (0, PATCH)))
    probe = lax.complex(probe_field[0], probe_field[1])
    slot_ids = jnp.arange(POSITIONS, dtype=jnp.int32)
    alive = (slot_ids % P_DEV < counts[slot_ids // P_DEV]).astype(jnp.float32)

    def visit(carry, item):
        gradient, probe_total = carry
        corner, measured, weight = item
        start_row = corner[0].astype(jnp.int32)
        start_col = corner[1].astype(jnp.int32)
        patches = lax.dynamic_slice(padded, (start_row, start_col), (PATCH, PATCH))
        exit_wave = probe * patches
        far = jnp.fft.fft2(exit_wave, norm='ortho')
        amplitude = jnp.sqrt(jnp.real(far) * jnp.real(far) + jnp.imag(far) * jnp.imag(far) + stabilizer)
        projected = far * (jnp.sqrt(measured) / amplitude)
        back = jnp.fft.ifft2(projected, norm='ortho')
        difference = (exit_wave - back) * weight
        current = lax.dynamic_slice(gradient, (start_row, start_col), (PATCH, PATCH))
        gradient = lax.dynamic_update_slice(gradient, current + jnp.conj(probe) * difference, (start_row, start_col))
        probe_total = probe_total + jnp.conj(patches) * difference
        return ((gradient, probe_total), None)
    start = (jnp.zeros_like(padded), jnp.zeros_like(probe))
    (gradient, probe_total), _ = lax.scan(visit, start, (offsets, intensity, alive))
    inside = gradient[:NY, :NX]
    object_grad = jnp.stack([jnp.real(inside), jnp.imag(inside)])
    probe_total = probe_total / jnp.sqrt(jnp.float32(POSITIONS))
    probe_grad = jnp.stack([jnp.real(probe_total), jnp.imag(probe_total)])
    return (object_grad, probe_grad)
```

```python
import functools
import math

import jax
import jax.numpy as jnp
import ml_dtypes
import numpy as np
from jax import lax
from jax.experimental import pallas as pl
from jax.experimental.pallas import tpu as pltpu
from jax.sharding import PartitionSpec as P

MESH = pl.DeviceIdType.MESH
f32 = jnp.float32
bf16 = jnp.bfloat16
stabilizer = 0.01
N = 256
TR = 256
TC = 512
SLOTS = 4
CH = 32


def dft_tables():
    index = np.arange(N)
    angles = (index[:, None] * index[None, :] % N) * (2.0 * np.pi / N)
    c = np.cos(angles) / math.sqrt(N)
    s = np.sin(angles) / math.sqrt(N)
    both = np.stack([np.block([[c, -s], [s, c]]), np.block([[c, s], [-s, c]])]).astype(np.float32)
    high = both.astype(ml_dtypes.bfloat16)
    low = (both - high.astype(np.float32)).astype(ml_dtypes.bfloat16)
    return np.stack([high, low], axis=1)


def rows(start, size):
    return pl.ds(pl.multiple_of(start, 8), size)


def split(value):
    high = value.astype(bf16)
    return high, (value - high.astype(f32)).astype(bf16)


def dot(a, b):
    return jnp.dot(a, b, preferred_element_type=f32)


def kernel(
    nrow, ncol,
    offs, cnt, obj, probe_in, inten_in, tab_in,
    grad_out, pg_out,
    ext, probe, inten, tab, Rs, Rt, Cs, Ct, rvec, cvec, lvec, cmask, Pw, Pc, X, Y, Pj, D, patch, ex, Tc, Uc, G, kbuf, lbuf, rbuf,
    pgl, crecv, H, yrecv, zsrc, zrecv, xbuf, res,
    local_sem, halo_send, halo_recv, core_send, core_recv, y_send, y_recv, z_send, z_recv, x_send, x_recv,
):
    ny, nz = nrow // 4, ncol // 2
    row, col = lax.axis_index("row"), lax.axis_index("col")
    y, x_lo, core = row // 4, (row // 2) % 2, row % 2
    x_hi, z = col // nz, col % nz
    x = x_hi * 2 + x_lo
    has_up, has_down = row > 0, row < nrow - 1
    has_left, has_right = col > 0, col < ncol - 1
    partner = row + 1 - 2 * core

    def y_peer(k):
        return lax.rem(y + k, ny)

    def z_peer(k):
        return lax.rem(z + k, nz)

    def x_peer(k):
        return lax.rem(x + k, 4)

    def y_id(k):
        return (y_peer(k) * 4 + x_lo * 2 + core, col)

    def z_id(k):
        return (row, x_hi * nz + z_peer(k))

    def x_id(k):
        other = x_peer(k)
        return (y * 4 + lax.rem(other, 2) * 2 + core, (other // 2) * nz + z)

    loads = [
        pltpu.make_async_copy(obj, ext.at[:, pl.ds(0, TR), pl.ds(0, TC)], local_sem.at[0]),
        pltpu.make_async_copy(probe_in, probe, local_sem.at[1]),
        pltpu.make_async_copy(inten_in, inten, local_sem.at[2]),
        pltpu.make_async_copy(tab_in, tab, local_sem.at[3]),
    ]
    loads[1].start()

    barrier = pltpu.get_barrier_semaphore()

    def greet(device):
        pl.semaphore_signal(barrier, inc=1, device_id=device, device_id_type=MESH)

    for k in range(1, ny):
        greet(y_id(k))
    for k in range(1, nz):
        greet(z_id(k))
    for k in range(1, 4):
        greet(x_id(k))
    far_right = has_right & (z == nz - 1)
    far_left = has_left & (z == 0)

    @pl.when(has_up)
    def _():
        greet((row - 1, col))

    @pl.when(has_down)
    def _():
        greet((row + 1, col))

    @pl.when(far_left)
    def _():
        greet((row, col - 1))

    @pl.when(far_right)
    def _():
        greet((row, col + 1))

    loads[0].start()
    loads[2].start()
    loads[3].start()
    one = lambda flag: flag.astype(jnp.int32)
    pl.semaphore_wait(barrier, ny + nz + 1 + one(has_up) + one(has_down) + one(far_left) + one(far_right))

    def halo(index, source, target, device):
        return pltpu.make_async_remote_copy(
            src_ref=source, dst_ref=target, send_sem=halo_send.at[index], recv_sem=halo_recv.at[index],
            device_id=device, device_id_type=MESH,
        )

    up_id = (lax.max(row - 1, 0), col)
    down_id = (lax.min(row + 1, nrow - 1), col)
    left_id = (row, lax.max(col - 1, 0))
    right_id = (row, lax.min(col + 1, ncol - 1))
    top, bottom = pl.ds(0, TR), pl.ds(TR, TR)
    main, side = pl.ds(0, TC), pl.ds(TC, N)
    right_in = halo(0, obj.at[:, :, pl.ds(0, N)], ext.at[:, top, side], left_id)
    lower_in = halo(1, obj, ext.at[:, bottom, main], up_id)
    corner_in = halo(2, ext.at[:, top, side], ext.at[:, bottom, side], up_id)

    @pl.when(has_left)
    def _():
        right_in.start()

    @pl.when(has_up)
    def _():
        lower_in.start()

    @pl.when(jnp.logical_not(has_right))
    def _():
        ext[:, :, TC:] = jnp.zeros((2, 2 * TR, N), f32)

    @pl.when(jnp.logical_not(has_down))
    def _():
        ext[:, TR:, :] = jnp.zeros((2, TR, TC + N), f32)

    @pl.when(jnp.logical_not(has_up))
    def _():
        kbuf[...] = jnp.zeros_like(kbuf)
        lbuf[...] = jnp.zeros_like(lbuf)

    @pl.when(jnp.logical_not(has_left))
    def _():
        rbuf[...] = jnp.zeros_like(rbuf)

    lanes = lax.broadcasted_iota(jnp.int32, (CH, N), 1)
    lines = lax.broadcasted_iota(jnp.int32, (CH, N), 0)

    def one_hot(flag):
        return jnp.where(flag, 1.0, 0.0).astype(bf16)

    for s in range(SLOTS):
        r = jnp.full((CH, N), offs[s, 0], jnp.int32) - row * TR
        c = jnp.full((CH, N), offs[s, 1], jnp.int32) - col * TC
        rvec[s] = r
        cvec[s] = c
        lvec[s] = jnp.where(jnp.full((CH, N), cnt[0], jnp.int32) > s, 1.0, 0.0)
        for b in range(3):
            cmask[s, b] = jnp.where((lanes + N * b >= c) & (lanes + N * b < c + N), 1.0, 0.0)[:8]

    def permutations(s, _):
        r, c = rvec[s], cvec[s]

        def body(i, _):
            line = lines + i * CH
            Rs[s, rows(i * CH, CH), :] = one_hot(line == ((lanes + r) & (N - 1)))
            Rt[s, rows(i * CH, CH), :] = one_hot(lanes == ((line + r) & (N - 1)))
            Cs[s, rows(i * CH, CH), :] = one_hot(lanes == ((line + c) & (N - 1)))
            Ct[s, rows(i * CH, CH), :] = one_hot(line == ((lanes + c) & (N - 1)))
            return 0

        lax.fori_loop(0, N // CH, body, 0)
        return 0

    lax.fori_loop(0, SLOTS, permutations, 0)

    loads[1].wait()

    def split_probe(i, _):
        here = rows(i * CH, CH)
        for q in range(2):
            high, low = split(probe[q, here, :])
            Pw[here, q * N:(q + 1) * N] = high
            Pw[here, (q + 2) * N:(q + 3) * N] = low
        return 0

    lax.fori_loop(0, N // CH, split_probe, 0)

    def shift_probe(s, _):
        a = dot(Rs[s], Pw[...])
        for p in range(4):
            Uc[p * N:(p + 1) * N, :] = a[:, p * N:(p + 1) * N].astype(bf16)
        a = dot(Uc[...], Cs[s])
        for q in range(2):
            Pc[s, q] = a[q * N:(q + 1) * N] + a[(q + 2) * N:(q + 3) * N]
        return 0

    lax.fori_loop(0, SLOTS, shift_probe, 0)

    @pl.when(has_right)
    def _():
        right_in.wait_recv()

        @pl.when(has_up)
        def _():
            corner_in.start()

    for load in (loads[0], loads[2], loads[3]):
        load.wait()

    @pl.when(has_down)
    def _():
        lower_in.wait_recv()

        @pl.when(has_right)
        def _():
            corner_in.wait_recv()

    def slot(s, _):
        def gather(i, _):
            i0 = i * CH
            from_below = lines + i0 < rvec[s]
            first, second = lanes >= cvec[s], lanes + N >= cvec[s]
            parts = []
            for q in range(2):
                u = ext[q, rows(i0, CH), :]
                v = ext[q, rows(i0 + TR, CH), :]
                blocks = [jnp.where(from_below, v[:, b * N:(b + 1) * N], u[:, b * N:(b + 1) * N]) for b in range(3)]
                w = jnp.where(first, blocks[0], jnp.where(second, blocks[1], blocks[2]))
                patch[s, q, rows(i0, CH), :] = w
                parts.append(w)
            pr, pi = Pc[s, 0, rows(i0, CH), :], Pc[s, 1, rows(i0, CH), :]
            waves = (pr * parts[0] - pi * parts[1], pr * parts[1] + pi * parts[0])
            for q, wave in enumerate(waves):
                ex[s, q, rows(i0, CH), :] = wave
                high, low = split(wave)
                X[s, rows(i0, CH), q * N:(q + 1) * N] = high
                X[s, rows(i0 + N, CH), q * N:(q + 1) * N] = low
            return 0

        lax.fori_loop(0, N // CH, gather, 0, unroll=8)
        a = dot(X[s], tab[0, 0])
        a = a[:N] + a[N:] + dot(X[s, :N], tab[0, 1])
        for q in range(2):
            high, low = split(a[:, q * N:(q + 1) * N])
            Y[s, q * N:(q + 1) * N, :N] = high
            Y[s, q * N:(q + 1) * N, N:] = low
        a = dot(tab[1, 0], Y[s])
        D[s] = a[:, :N] + a[:, N:] + dot(tab[1, 1], Y[s, :, :N])

        def project(i, _):
            i0 = i * CH
            zr, zi = D[s, rows(i0, CH), :], D[s, rows(i0 + N, CH), :]
            measured = inten[s, rows(i0, CH), :]
            factor = measured * lax.rsqrt(measured * (zr * zr + zi * zi + stabilizer))
            for q, wave in enumerate((zr * factor, zi * factor)):
                high, low = split(wave)
                Pj[s, rows(i0 + q * N, CH), :N] = high
                Pj[s, rows(i0 + q * N, CH), N:] = low
            return 0

        lax.fori_loop(0, N // CH, project, 0, unroll=8)
        a = dot(tab[0, 0], Pj[s])
        a = a[:, :N] + a[:, N:] + dot(tab[0, 1], Pj[s, :, :N])
        for q in range(2):
            high, low = split(a[q * N:(q + 1) * N])
            X[s, :N, q * N:(q + 1) * N] = high
            X[s, N:, q * N:(q + 1) * N] = low
        a = dot(X[s], tab[1, 0])
        a = a[:N] + a[N:] + dot(X[s, :N], tab[1, 1])
        D[s, :N] = a[:, :N]
        D[s, N:] = a[:, N:]

        def finish(i, _):
            i0 = i * CH
            here, below = rows(i0, CH), rows(i0 + N, CH)
            live = lvec[s]
            dr = (ex[s, 0, here, :] - D[s, here, :]) * live
            di = (ex[s, 1, here, :] - D[s, below, :]) * live
            wr, wi = patch[s, 0, here, :], patch[s, 1, here, :]
            for q, term in enumerate((wr * dr + wi * di, wr * di - wi * dr)):
                high, low = split(term)
                Tc[here, q * N:(q + 1) * N] = high
                Tc[here, (q + 2) * N:(q + 3) * N] = low
            pr, pi = Pc[s, 0, here, :], Pc[s, 1, here, :]
            ex[s, 0, here, :] = pr * dr + pi * di
            ex[s, 1, here, :] = pr * di - pi * dr
            return 0

        lax.fori_loop(0, N // CH, finish, 0, unroll=8)

        a = dot(Rt[s], Tc[...])
        for q in range(2):
            high, low = split(a[:, q * N:(q + 1) * N] + a[:, (q + 2) * N:(q + 3) * N])
            Uc[q * N:(q + 1) * N, :] = high
            Uc[(q + 2) * N:(q + 3) * N, :] = low
        a = dot(Uc[...], Ct[s])
        for q in range(2):
            pgl[q] += a[q * N:(q + 1) * N] + a[(q + 2) * N:(q + 3) * N]
        return 0

    pgl[...] = jnp.zeros_like(pgl)
    lax.fori_loop(0, SLOTS, slot, 0)

    def deposit(i, _):
        i0 = i * 8
        here, below = rows(i0, 8), rows(i0 + N, 8)
        for q in range(2):
            terms = [ex[s, q, here, :] for s in range(SLOTS)]
            lower = [jnp.where(lines[:8] + i0 < rvec[s, :8], terms[s], 0.0) for s in range(SLOTS)]
            upper = [terms[s] - lower[s] for s in range(SLOTS)]
            for b in range(3):
                for part, target in ((lower, below), (upper, here)):
                    kept = [part[s] * cmask[s, b] for s in range(SLOTS)]
                    G[q, target, b * N:(b + 1) * N] = (kept[0] + kept[1]) + (kept[2] + kept[3])
        return 0

    lax.fori_loop(0, N // 8, deposit, 0, unroll=4)

    corner_out = halo(3, G.at[:, bottom, side], kbuf, down_id)
    lower_out = halo(4, G.at[:, bottom, main], lbuf, down_id)
    right_out = halo(5, G.at[:, top, side], rbuf, right_id)

    @pl.when(has_down)
    def _():
        corner_out.start()
        lower_out.start()

    def remote(source, target, send, recv, device):
        return pltpu.make_async_remote_copy(
            src_ref=source, dst_ref=target, send_sem=send, recv_sem=recv, device_id=device, device_id_type=MESH
        )

    to_partner = remote(pgl.at[1 - core], crecv, core_send.at[0], core_recv.at[0], (partner, col))
    to_partner.start()
    to_partner.wait_recv()

    def add_core(i, _):
        H[rows(i * CH, CH), :] = pgl[core, rows(i * CH, CH), :] + crecv[rows(i * CH, CH), :]
        return 0

    lax.fori_loop(0, N // CH, add_core, 0, unroll=8)
    ystep = N // ny
    y_out = [
        remote(H.at[rows(y_peer(k) * ystep, ystep), :], yrecv.at[k], y_send.at[k], y_recv.at[k], y_id(k)) for k in range(1, ny)
    ]
    for copy in y_out:
        copy.start()

    @pl.when(has_up)
    def _():
        corner_out.wait_recv()

    def add_corner(i, _):
        for q in range(2):
            G[q, rows(i * CH, CH), TC:] += kbuf[q, rows(i * CH, CH), :]
        return 0

    lax.fori_loop(0, TR // CH, add_corner, 0, unroll=8)

    @pl.when(has_right)
    def _():
        right_out.start()

    for copy in y_out:
        copy.wait_recv()
    summed = H[rows(y * ystep, ystep), :]
    for k in range(1, ny):
        summed = summed + yrecv[k]
    for p in range(nz):
        zsrc[p] = summed[8 * (p // 2):8 * (p // 2) + 8, 128 * (p % 2):128 * (p % 2) + 128]
    z_out = [remote(zsrc.at[z_peer(k)], zrecv.at[k], z_send.at[k], z_recv.at[k], z_id(k)) for k in range(1, nz)]
    for copy in z_out:
        copy.start()
    for copy in z_out:
        copy.wait_recv()
    tile = zsrc[z]
    for k in range(1, nz):
        tile = tile + zrecv[k]
    xbuf[x] = tile
    x_out = [remote(xbuf.at[x], xbuf.at[x], x_send.at[k], x_recv.at[k], x_id(k)) for k in range(1, 4)]
    for copy in x_out:
        copy.start()
    for copy in x_out:
        copy.wait_recv()
    tile = ((xbuf[0] + xbuf[1]) + (xbuf[2] + xbuf[3])) * f32(1.0 / math.sqrt(SLOTS * nrow * ncol))
    my_tile = (core, rows(y * ystep + 8 * (z // 2), 8), pl.ds(pl.multiple_of(128 * (z % 2), 128), 128))
    res[my_tile] = tile
    z_back = [remote(res.at[my_tile], res.at[my_tile], z_send.at[nz + k], z_recv.at[nz + k], z_id(k)) for k in range(1, nz)]
    for copy in z_back:
        copy.start()
    for copy in z_back:
        copy.wait_recv()
    my_rows = (core, rows(y * ystep, ystep))
    y_back = [remote(res.at[my_rows], res.at[my_rows], y_send.at[ny + k], y_recv.at[ny + k], y_id(k)) for k in range(1, ny)]
    for copy in y_back:
        copy.start()
    for copy in y_back:
        copy.wait_recv()
    share = remote(res.at[core], res.at[core], core_send.at[1], core_recv.at[1], (partner, col))
    share.start()

    @pl.when(has_up)
    def _():
        lower_out.wait_recv()

    @pl.when(has_left)
    def _():
        right_out.wait_recv()

    def add_halos(i, _):
        here = rows(i * CH, CH)
        for q in range(2):
            G[q, here, :N] = G[q, here, :N] + lbuf[q, here, :N] + rbuf[q, here, :]
            G[q, here, N:TC] = G[q, here, N:TC] + lbuf[q, here, N:]
        return 0

    lax.fori_loop(0, TR // CH, add_halos, 0, unroll=8)
    store_grad = pltpu.make_async_copy(G.at[:, top, main], grad_out, local_sem.at[4])
    store_grad.start()
    share.wait_recv()
    store_probe = pltpu.make_async_copy(res, pg_out, local_sem.at[5])
    store_probe.start()

    @pl.when(has_left)
    def _():
        right_in.wait_send()

    @pl.when(has_up)
    def _():
        lower_in.wait_send()

        @pl.when(has_right)
        def _():
            corner_in.wait_send()

    @pl.when(has_down)
    def _():
        corner_out.wait_send()
        lower_out.wait_send()

    @pl.when(has_right)
    def _():
        right_out.wait_send()

    to_partner.wait_send()
    share.wait_send()
    for copy in y_out + z_out + x_out + z_back + y_back:
        copy.wait_send()
    store_grad.wait()
    store_probe.wait()


def local(nrow, ncol, object_field, probe_field, intensity, offsets, counts):
    ny, nz = nrow // 4, ncol // 2
    anywhere = pl.BlockSpec(memory_space=pl.ANY)
    scalars = pl.BlockSpec(memory_space=pltpu.SMEM)
    vmem = pltpu.VMEM
    dma = pltpu.SemaphoreType.DMA
    grad, probe_grad = pl.pallas_call(
        functools.partial(kernel, nrow, ncol),
        out_shape=[jax.ShapeDtypeStruct((2, TR, TC), f32), jax.ShapeDtypeStruct((2, N, N), f32)],
        in_specs=[scalars, scalars] + [anywhere] * 4,
        out_specs=[anywhere, anywhere],
        scratch_shapes=[
            vmem((2, 2 * TR, TC + N), f32),
            vmem((2, N, N), f32),
            vmem((SLOTS, N, N), f32),
            vmem((2, 2, 2 * N, 2 * N), bf16),
            vmem((SLOTS, N, N), bf16),
            vmem((SLOTS, N, N), bf16),
            vmem((SLOTS, N, N), bf16),
            vmem((SLOTS, N, N), bf16),
            vmem((SLOTS, CH, N), jnp.int32),
            vmem((SLOTS, CH, N), jnp.int32),
            vmem((SLOTS, CH, N), f32),
            vmem((SLOTS, 3, 8, N), f32),
            vmem((N, 4 * N), bf16),
            vmem((SLOTS, 2, N, N), f32),
            vmem((SLOTS, 2 * N, 2 * N), bf16),
            vmem((SLOTS, 2 * N, 2 * N), bf16),
            vmem((SLOTS, 2 * N, 2 * N), bf16),
            vmem((SLOTS, 2 * N, N), f32),
            vmem((SLOTS, 2, N, N), f32),
            vmem((SLOTS, 2, N, N), f32),
            vmem((N, 4 * N), bf16),
            vmem((4 * N, N), bf16),
            vmem((2, 2 * TR, TC + N), f32),
            vmem((2, TR, N), f32),
            vmem((2, TR, TC), f32),
            vmem((2, TR, N), f32),
            vmem((2, N, N), f32),
            vmem((N, N), f32),
            vmem((N, N), f32),
            vmem((ny, N // ny, N), f32),
            vmem((nz, 8, 128), f32),
            vmem((nz, 8, 128), f32),
            vmem((4, 8, 128), f32),
            vmem((2, N, N), f32),
            dma((6,)), dma((6,)), dma((6,)), dma((2,)), dma((2,)),
            dma((2 * ny,)), dma((2 * ny,)), dma((2 * nz,)), dma((2 * nz,)), dma((4,)), dma((4,)),
        ],
        compiler_params=pltpu.CompilerParams(collective_id=0, has_side_effects=True, vmem_limit_bytes=56 * 2**20),
    )(offsets, counts, object_field, probe_field, intensity, jnp.asarray(dft_tables()))
    return grad, probe_grad


def solution(mesh):
    in_specs = (
        P(None, "row", "col"),
        P(),
        P(("row", "col"), None, None),
        P(("row", "col"), None),
        P(("row", "col")),
    )
    out_specs = (P(None, "row", "col"), P())
    body = functools.partial(local, mesh.shape["row"], mesh.shape["col"])
    return jax.shard_map(body, mesh=mesh, in_specs=in_specs, out_specs=out_specs, check_vma=False)
```

```python
import functools
import math

import jax
import jax.numpy as jnp
import ml_dtypes
import numpy as np
from jax import lax
from jax.experimental import pallas as pl
from jax.experimental.pallas import tpu as pltpu
from jax.sharding import PartitionSpec as P

MESH = pl.DeviceIdType.MESH
f32 = jnp.float32
bf16 = jnp.bfloat16
stabilizer = 0.01
N = 256
TR = 256
TC = 512
SLOTS = 4
CH = 32


def dft_tables():
    index = np.arange(N)
    angles = (index[:, None] * index[None, :] % N) * (2.0 * np.pi / N)
    c = np.cos(angles) / math.sqrt(N)
    s = np.sin(angles) / math.sqrt(N)
    both = np.stack([np.block([[c, -s], [s, c]]), np.block([[c, s], [-s, c]])]).astype(np.float32)
    high = both.astype(ml_dtypes.bfloat16)
    low = (both - high.astype(np.float32)).astype(ml_dtypes.bfloat16)
    return np.stack([high, low], axis=1)


def rows(start, size):
    return pl.ds(pl.multiple_of(start, 8), size)


def split(value):
    high = value.astype(bf16)
    return high, (value - high.astype(f32)).astype(bf16)


def dot(a, b):
    return jnp.dot(a, b, preferred_element_type=f32)


def kernel(
    nrow, ncol,
    offs, cnt, obj, probe_in, inten_in, tab_in,
    grad_out, pg_out,
    ext, probe, inten, tab, Rs, Rt, Cs, Ct, rvec, cvec, lvec, cmask, Pw, Pc, X, Y, Pj, D, patch, ex, Tc, Uc, G, kbuf, lbuf, rbuf,
    pgl, crecv, H, zrecv, ysrc, yrecv, xbuf, res,
    local_sem, halo_send, halo_recv, core_send, core_recv, y_send, y_recv, z_send, z_recv, x_send, x_recv,
):
    ny, nz = nrow // 4, ncol // 2
    row, col = lax.axis_index("row"), lax.axis_index("col")
    y, x_lo, core = row // 4, (row // 2) % 2, row % 2
    x_hi, z = col // nz, col % nz
    x = x_hi * 2 + x_lo
    has_up, has_down = row > 0, row < nrow - 1
    has_left, has_right = col > 0, col < ncol - 1
    partner = row + 1 - 2 * core

    def y_peer(k):
        return lax.rem(y + k, ny)

    def z_peer(k):
        return lax.rem(z + k, nz)

    def x_peer(k):
        return lax.rem(x + k, 4)

    def y_id(k):
        return (y_peer(k) * 4 + x_lo * 2 + core, col)

    def z_id(k):
        return (row, x_hi * nz + z_peer(k))

    def x_id(k):
        other = x_peer(k)
        return (y * 4 + lax.rem(other, 2) * 2 + core, (other // 2) * nz + z)

    loads = [
        pltpu.make_async_copy(obj, ext.at[:, pl.ds(0, TR), pl.ds(0, TC)], local_sem.at[0]),
        pltpu.make_async_copy(probe_in, probe, local_sem.at[1]),
        pltpu.make_async_copy(inten_in, inten, local_sem.at[2]),
        pltpu.make_async_copy(tab_in, tab, local_sem.at[3]),
    ]
    loads[1].start()

    barrier = pltpu.get_barrier_semaphore()

    def greet(device):
        pl.semaphore_signal(barrier, inc=1, device_id=device, device_id_type=MESH)

    for k in range(1, ny):
        greet(y_id(k))
    for k in range(1, nz):
        greet(z_id(k))
    for k in range(1, 4):
        greet(x_id(k))
    far_right = has_right & (z == nz - 1)
    far_left = has_left & (z == 0)

    @pl.when(has_up)
    def _():
        greet((row - 1, col))

    @pl.when(has_down)
    def _():
        greet((row + 1, col))

    @pl.when(far_left)
    def _():
        greet((row, col - 1))

    @pl.when(far_right)
    def _():
        greet((row, col + 1))

    loads[0].start()
    loads[2].start()
    loads[3].start()
    one = lambda flag: flag.astype(jnp.int32)
    pl.semaphore_wait(barrier, ny + nz + 1 + one(has_up) + one(has_down) + one(far_left) + one(far_right))

    def halo(index, source, target, device):
        return pltpu.make_async_remote_copy(
            src_ref=source, dst_ref=target, send_sem=halo_send.at[index], recv_sem=halo_recv.at[index],
            device_id=device, device_id_type=MESH,
        )

    up_id = (lax.max(row - 1, 0), col)
    down_id = (lax.min(row + 1, nrow - 1), col)
    left_id = (row, lax.max(col - 1, 0))
    right_id = (row, lax.min(col + 1, ncol - 1))
    top, bottom = pl.ds(0, TR), pl.ds(TR, TR)
    main, side = pl.ds(0, TC), pl.ds(TC, N)
    half = TR // 2
    halves = (pl.ds(0, half), pl.ds(half, half))
    right_in = [
        halo(0, obj.at[:, halves[0], pl.ds(0, N)], ext.at[:, halves[0], side], left_id),
        halo(6, obj.at[:, halves[1], pl.ds(0, N)], ext.at[:, halves[1], side], left_id),
    ]
    lower_in = halo(1, obj, ext.at[:, bottom, main], up_id)
    corner_in = halo(2, ext.at[:, top, side], ext.at[:, bottom, side], up_id)

    @pl.when(has_left)
    def _():
        right_in[0].start()
        right_in[1].start()

    @pl.when(has_up)
    def _():
        lower_in.start()

    @pl.when(jnp.logical_not(has_right))
    def _():
        ext[:, :, TC:] = jnp.zeros((2, 2 * TR, N), f32)

    @pl.when(jnp.logical_not(has_down))
    def _():
        ext[:, TR:, :] = jnp.zeros((2, TR, TC + N), f32)

    @pl.when(jnp.logical_not(has_up))
    def _():
        kbuf[...] = jnp.zeros_like(kbuf)
        lbuf[...] = jnp.zeros_like(lbuf)

    @pl.when(jnp.logical_not(has_left))
    def _():
        rbuf[...] = jnp.zeros_like(rbuf)

    lanes = lax.broadcasted_iota(jnp.int32, (CH, N), 1)
    lines = lax.broadcasted_iota(jnp.int32, (CH, N), 0)

    def one_hot(flag):
        return jnp.where(flag, 1.0, 0.0).astype(bf16)

    for s in range(SLOTS):
        r = jnp.full((CH, N), offs[0, s], jnp.int32) - row * TR
        c = jnp.full((CH, N), offs[1, s], jnp.int32) - col * TC
        rvec[s] = r
        cvec[s] = c
        lvec[s] = jnp.where(jnp.full((CH, N), cnt[0], jnp.int32) > s, 1.0, 0.0)
        for b in range(3):
            cmask[s, b] = jnp.where((lanes + N * b >= c) & (lanes + N * b < c + N), 1.0, 0.0)[:8]

    def permutations(s, _):
        r, c = rvec[s], cvec[s]

        def body(i, _):
            line = lines + i * CH
            Rs[s, rows(i * CH, CH), :] = one_hot(line == ((lanes + r) & (N - 1)))
            Rt[s, rows(i * CH, CH), :] = one_hot(lanes == ((line + r) & (N - 1)))
            Cs[s, rows(i * CH, CH), :] = one_hot(lanes == ((line + c) & (N - 1)))
            Ct[s, rows(i * CH, CH), :] = one_hot(line == ((lanes + c) & (N - 1)))
            return 0

        lax.fori_loop(0, N // CH, body, 0)
        return 0

    lax.fori_loop(0, SLOTS, permutations, 0)

    loads[1].wait()

    def split_probe(i, _):
        here = rows(i * CH, CH)
        for q in range(2):
            high, low = split(probe[q, here, :])
            Pw[here, q * N:(q + 1) * N] = high
            Pw[here, (q + 2) * N:(q + 3) * N] = low
        return 0

    lax.fori_loop(0, N // CH, split_probe, 0)

    def shift_probe(s, _):
        a = dot(Rs[s], Pw[...])
        for p in range(4):
            Uc[p * N:(p + 1) * N, :] = a[:, p * N:(p + 1) * N].astype(bf16)
        a = dot(Uc[...], Cs[s])
        for q in range(2):
            Pc[s, q] = a[q * N:(q + 1) * N] + a[(q + 2) * N:(q + 3) * N]
        return 0

    lax.fori_loop(0, SLOTS, shift_probe, 0)

    @pl.when(has_right)
    def _():
        right_in[0].wait_recv()
        right_in[1].wait_recv()

        @pl.when(has_up)
        def _():
            corner_in.start()

    for load in (loads[0], loads[2], loads[3]):
        load.wait()

    @pl.when(has_down)
    def _():
        lower_in.wait_recv()

        @pl.when(has_right)
        def _():
            corner_in.wait_recv()

    def slot(s, _):
        def gather(i, _):
            i0 = i * CH
            from_below = lines + i0 < rvec[s]
            first, second = lanes >= cvec[s], lanes + N >= cvec[s]
            parts = []
            for q in range(2):
                u = ext[q, rows(i0, CH), :]
                v = ext[q, rows(i0 + TR, CH), :]
                blocks = [jnp.where(from_below, v[:, b * N:(b + 1) * N], u[:, b * N:(b + 1) * N]) for b in range(3)]
                w = jnp.where(first, blocks[0], jnp.where(second, blocks[1], blocks[2]))
                patch[s, q, rows(i0, CH), :] = w
                parts.append(w)
            pr, pi = Pc[s, 0, rows(i0, CH), :], Pc[s, 1, rows(i0, CH), :]
            waves = (pr * parts[0] - pi * parts[1], pr * parts[1] + pi * parts[0])
            for q, wave in enumerate(waves):
                ex[s, q, rows(i0, CH), :] = wave
                high, low = split(wave)
                X[s, rows(i0, CH), q * N:(q + 1) * N] = high
                X[s, rows(i0 + N, CH), q * N:(q + 1) * N] = low
            return 0

        lax.fori_loop(0, N // CH, gather, 0, unroll=8)
        a = dot(X[s], tab[0, 0])
        a = a[:N] + a[N:] + dot(X[s, :N], tab[0, 1])
        for q in range(2):
            high, low = split(a[:, q * N:(q + 1) * N])
            Y[s, q * N:(q + 1) * N, :N] = high
            Y[s, q * N:(q + 1) * N, N:] = low
        a = dot(tab[1, 0], Y[s])
        D[s] = a[:, :N] + a[:, N:] + dot(tab[1, 1], Y[s, :, :N])

        def project(i, _):
            i0 = i * CH
            zr, zi = D[s, rows(i0, CH), :], D[s, rows(i0 + N, CH), :]
            measured = inten[s, rows(i0, CH), :]
            factor = measured * lax.rsqrt(measured * (zr * zr + zi * zi + stabilizer))
            for q, wave in enumerate((zr * factor, zi * factor)):
                high, low = split(wave)
                Pj[s, rows(i0 + q * N, CH), :N] = high
                Pj[s, rows(i0 + q * N, CH), N:] = low
            return 0

        lax.fori_loop(0, N // CH, project, 0, unroll=8)
        a = dot(tab[0, 0], Pj[s])
        a = a[:, :N] + a[:, N:] + dot(tab[0, 1], Pj[s, :, :N])
        for q in range(2):
            high, low = split(a[q * N:(q + 1) * N])
            X[s, :N, q * N:(q + 1) * N] = high
            X[s, N:, q * N:(q + 1) * N] = low
        a = dot(X[s], tab[1, 0])
        a = a[:N] + a[N:] + dot(X[s, :N], tab[1, 1])
        D[s, :N] = a[:, :N]
        D[s, N:] = a[:, N:]

        def finish(i, _):
            i0 = i * CH
            here, below = rows(i0, CH), rows(i0 + N, CH)
            live = lvec[s]
            dr = (ex[s, 0, here, :] - D[s, here, :]) * live
            di = (ex[s, 1, here, :] - D[s, below, :]) * live
            wr, wi = patch[s, 0, here, :], patch[s, 1, here, :]
            for q, term in enumerate((wr * dr + wi * di, wr * di - wi * dr)):
                high, low = split(term)
                Tc[here, q * N:(q + 1) * N] = high
                Tc[here, (q + 2) * N:(q + 3) * N] = low
            pr, pi = Pc[s, 0, here, :], Pc[s, 1, here, :]
            ex[s, 0, here, :] = pr * dr + pi * di
            ex[s, 1, here, :] = pr * di - pi * dr
            return 0

        lax.fori_loop(0, N // CH, finish, 0, unroll=8)

        a = dot(Rt[s], Tc[...])
        for q in range(2):
            high, low = split(a[:, q * N:(q + 1) * N] + a[:, (q + 2) * N:(q + 3) * N])
            Uc[q * N:(q + 1) * N, :] = high
            Uc[(q + 2) * N:(q + 3) * N, :] = low
        a = dot(Uc[...], Ct[s])
        for q in range(2):
            pgl[q] += a[q * N:(q + 1) * N] + a[(q + 2) * N:(q + 3) * N]
        return 0

    pgl[...] = jnp.zeros_like(pgl)
    lax.fori_loop(0, SLOTS, slot, 0)

    def remote(source, target, send, recv, device):
        return pltpu.make_async_remote_copy(
            src_ref=source, dst_ref=target, send_sem=send, recv_sem=recv, device_id=device, device_id_type=MESH
        )

    to_partner = remote(pgl.at[1 - core], crecv, core_send.at[0], core_recv.at[0], (partner, col))
    to_partner.start()

    def deposit(i, _):
        i0 = i * 8
        here, below = rows(i0, 8), rows(i0 + N, 8)
        for q in range(2):
            terms = [ex[s, q, here, :] for s in range(SLOTS)]
            lower = [jnp.where(lines[:8] + i0 < rvec[s, :8], terms[s], 0.0) for s in range(SLOTS)]
            upper = [terms[s] - lower[s] for s in range(SLOTS)]
            for b in range(3):
                for part, target in ((lower, below), (upper, here)):
                    kept = [part[s] * cmask[s, b] for s in range(SLOTS)]
                    G[q, target, b * N:(b + 1) * N] = (kept[0] + kept[1]) + (kept[2] + kept[3])
        return 0

    lax.fori_loop(0, N // 8, deposit, 0, unroll=4)

    corner_out = halo(3, G.at[:, bottom, side], kbuf, down_id)
    lower_out = halo(4, G.at[:, bottom, main], lbuf, down_id)
    right_out = [
        halo(5, G.at[:, halves[0], side], rbuf.at[:, halves[0], :], right_id),
        halo(8, G.at[:, halves[1], side], rbuf.at[:, halves[1], :], right_id),
    ]

    @pl.when(has_down)
    def _():
        corner_out.start()
        lower_out.start()

    to_partner.wait_recv()

    def add_core(i, _):
        for p in range(nz):
            here = rows(i * nz * 8 + p * 8, 8)
            H[i, p] = pgl[core, here, :] + crecv[here, :]
        return 0

    lax.fori_loop(0, N // (8 * nz), add_core, 0, unroll=True)
    z_out = [remote(H.at[:, z_peer(k)], zrecv.at[k], z_send.at[k], z_recv.at[k], z_id(k)) for k in range(1, nz)]
    for copy in z_out:
        copy.start()

    for copy in z_out:
        copy.wait_recv()
    for a in range(N // (8 * nz)):
        summed = H[a, z]
        for k in range(1, nz):
            summed = summed + zrecv[k, a]
        for half in range(2):
            ysrc[2 * a + half] = summed[:, 128 * half:128 * half + 128]
    y_out = [remote(ysrc.at[y_peer(k)], yrecv.at[k], y_send.at[k], y_recv.at[k], y_id(k)) for k in range(1, ny)]
    for copy in y_out:
        copy.start()
    @pl.when(has_up)
    def _():
        corner_out.wait_recv()

    def add_corner(i, _):
        for q in range(2):
            G[q, rows(i * CH, CH), TC:] += kbuf[q, rows(i * CH, CH), :]
        return 0

    lax.fori_loop(0, TR // CH, add_corner, 0, unroll=8)

    @pl.when(has_right)
    def _():
        right_out[0].start()
        right_out[1].start()

    for copy in y_out:
        copy.wait_recv()
    tile = ysrc[y]
    for k in range(1, ny):
        tile = tile + yrecv[k]
    xbuf[x] = tile
    x_out = [remote(xbuf.at[x], xbuf.at[x], x_send.at[k], x_recv.at[k], x_id(k)) for k in range(1, 4)]
    for copy in x_out:
        copy.start()
    for copy in x_out:
        copy.wait_recv()
    tile = ((xbuf[0] + xbuf[1]) + (xbuf[2] + xbuf[3])) * f32(1.0 / math.sqrt(SLOTS * nrow * ncol))
    my_lanes = pl.ds(pl.multiple_of(128 * (y % 2), 128), 128)
    my_tile = (core, rows(8 * nz * (y // 2) + 8 * z, 8), my_lanes)
    res[my_tile] = tile
    z_back = [remote(res.at[my_tile], res.at[my_tile], z_send.at[nz + k], z_recv.at[nz + k], z_id(k)) for k in range(1, nz)]
    for copy in z_back:
        copy.start()

    for copy in z_back:
        copy.wait_recv()
    my_rows = (core, rows(8 * nz * (y // 2), 8 * nz), my_lanes)
    y_back = [remote(res.at[my_rows], res.at[my_rows], y_send.at[ny + k], y_recv.at[ny + k], y_id(k)) for k in range(1, ny)]
    for copy in y_back:
        copy.start()
    for copy in y_back:
        copy.wait_recv()
    share = remote(res.at[core], res.at[core], core_send.at[1], core_recv.at[1], (partner, col))
    share.start()

    @pl.when(has_up)
    def _():
        lower_out.wait_recv()

    @pl.when(has_left)
    def _():
        right_out[0].wait_recv()
        right_out[1].wait_recv()

    def add_halos(i, _):
        here = rows(i * CH, CH)
        for q in range(2):
            G[q, here, :N] = G[q, here, :N] + lbuf[q, here, :N] + rbuf[q, here, :]
            G[q, here, N:TC] = G[q, here, N:TC] + lbuf[q, here, N:]
        return 0

    lax.fori_loop(0, TR // CH, add_halos, 0, unroll=8)
    store_grad = pltpu.make_async_copy(G.at[:, top, main], grad_out, local_sem.at[4])
    store_grad.start()
    share.wait_recv()
    store_probe = pltpu.make_async_copy(res, pg_out, local_sem.at[5])
    store_probe.start()

    @pl.when(has_left)
    def _():
        right_in[0].wait_send()
        right_in[1].wait_send()

    @pl.when(has_up)
    def _():
        lower_in.wait_send()

        @pl.when(has_right)
        def _():
            corner_in.wait_send()

    @pl.when(has_down)
    def _():
        corner_out.wait_send()
        lower_out.wait_send()

    @pl.when(has_right)
    def _():
        right_out[0].wait_send()
        right_out[1].wait_send()

    to_partner.wait_send()
    share.wait_send()
    for copy in y_out + z_out + x_out + z_back + y_back:
        copy.wait_send()
    store_grad.wait()
    store_probe.wait()


def local(nrow, ncol, object_field, probe_field, intensity, offsets, counts):
    ny, nz = nrow // 4, ncol // 2
    anywhere = pl.BlockSpec(memory_space=pl.ANY)
    scalars = pl.BlockSpec(memory_space=pltpu.SMEM)
    vmem = pltpu.VMEM
    dma = pltpu.SemaphoreType.DMA
    grad, probe_grad = pl.pallas_call(
        functools.partial(kernel, nrow, ncol),
        out_shape=[jax.ShapeDtypeStruct((2, TR, TC), f32), jax.ShapeDtypeStruct((2, N, N), f32)],
        in_specs=[scalars, scalars] + [anywhere] * 4,
        out_specs=[anywhere, anywhere],
        scratch_shapes=[
            vmem((2, 2 * TR, TC + N), f32),
            vmem((2, N, N), f32),
            vmem((SLOTS, N, N), f32),
            vmem((2, 2, 2 * N, 2 * N), bf16),
            vmem((SLOTS, N, N), bf16),
            vmem((SLOTS, N, N), bf16),
            vmem((SLOTS, N, N), bf16),
            vmem((SLOTS, N, N), bf16),
            vmem((SLOTS, CH, N), jnp.int32),
            vmem((SLOTS, CH, N), jnp.int32),
            vmem((SLOTS, CH, N), f32),
            vmem((SLOTS, 3, 8, N), f32),
            vmem((N, 4 * N), bf16),
            vmem((SLOTS, 2, N, N), f32),
            vmem((SLOTS, 2 * N, 2 * N), bf16),
            vmem((SLOTS, 2 * N, 2 * N), bf16),
            vmem((SLOTS, 2 * N, 2 * N), bf16),
            vmem((SLOTS, 2 * N, N), f32),
            vmem((SLOTS, 2, N, N), f32),
            vmem((SLOTS, 2, N, N), f32),
            vmem((N, 4 * N), bf16),
            vmem((4 * N, N), bf16),
            vmem((2, 2 * TR, TC + N), f32),
            vmem((2, TR, N), f32),
            vmem((2, TR, TC), f32),
            vmem((2, TR, N), f32),
            vmem((2, N, N), f32),
            vmem((N, N), f32),
            vmem((N // (8 * nz), nz, 8, N), f32),
            vmem((nz, N // (8 * nz), 8, N), f32),
            vmem((ny, 8, 128), f32),
            vmem((ny, 8, 128), f32),
            vmem((4, 8, 128), f32),
            vmem((2, N, N), f32),
            dma((6,)), dma((9,)), dma((9,)), dma((2,)), dma((2,)),
            dma((2 * ny,)), dma((2 * ny,)), dma((2 * nz,)), dma((2 * nz,)), dma((4,)), dma((4,)),
        ],
        compiler_params=pltpu.CompilerParams(collective_id=0, has_side_effects=True, vmem_limit_bytes=56 * 2**20),
    )(offsets.T, counts, object_field, probe_field, intensity, jnp.asarray(dft_tables()))
    return grad, probe_grad


def solution(mesh):
    in_specs = (
        P(None, "row", "col"),
        P(),
        P(("row", "col"), None, None),
        P(("row", "col"), None),
        P(("row", "col")),
    )
    out_specs = (P(None, "row", "col"), P())
    body = functools.partial(local, mesh.shape["row"], mesh.shape["col"])
    return jax.shard_map(body, mesh=mesh, in_specs=in_specs, out_specs=out_specs, check_vma=False)
```

```python
import functools
import math

import jax
import jax.numpy as jnp
import ml_dtypes
import numpy as np
from jax import lax
from jax.experimental import pallas as pl
from jax.experimental.pallas import tpu as pltpu
from jax.sharding import PartitionSpec as P

MESH = pl.DeviceIdType.MESH
f32 = jnp.float32
bf16 = jnp.bfloat16
stabilizer = 0.01
N = 256
TR = 256
TC = 512
SLOTS = 4
CH = 32
M = N // 2


def dft_tables():
    index = np.arange(M)
    angles = (index[:, None] * index[None, :] % M) * (2.0 * np.pi / M)
    c = np.cos(angles) / math.sqrt(N)
    s = np.sin(angles) / math.sqrt(N)
    both = np.stack([np.block([[c, -s], [s, c]]), np.block([[c, s], [-s, c]])]).astype(np.float32)
    high = both.astype(ml_dtypes.bfloat16)
    low = (both - high.astype(np.float32)).astype(ml_dtypes.bfloat16)
    return np.stack([high, low], axis=1)


def twiddles():
    angles = np.arange(M) * (2.0 * np.pi / N)
    pair = np.stack([np.cos(angles), np.sin(angles)]).astype(np.float32)
    return np.broadcast_to(pair[:, :, None], (2, M, N)).copy(), np.broadcast_to(pair[:, None, :], (2, N, M)).copy()


def rows(start, size):
    return pl.ds(pl.multiple_of(start, 8), size)


def split(value):
    high = value.astype(bf16)
    return high, (value - high.astype(f32)).astype(bf16)


def dot(a, b):
    return jnp.dot(a, b, preferred_element_type=f32)


def forward_half(tops, bottoms, cosine, sine):
    real, imag = tops[0] - bottoms[0], tops[1] - bottoms[1]
    odd = (real * cosine + imag * sine, imag * cosine - real * sine)
    return (tops[0] + bottoms[0], tops[1] + bottoms[1]), odd


def backward_half(even, odd, cosine, sine):
    real, imag = odd[0] * cosine - odd[1] * sine, odd[0] * sine + odd[1] * cosine
    return (even[0] + real, even[1] + imag), (even[0] - real, even[1] - imag)


def kernel(
    nrow, ncol,
    offs, cnt, obj, probe_in, inten_in, tab_in, row_turn_in, lane_turn_in,
    grad_out, pg_out,
    ext, probe, inten, tab, row_turn, lane_turn, Ip, Rs, Rt, Cs, Ct, rvec, cvec, lvec, cmask, Pw, Pc, X, Y, Pj, D, B, patch, ex, Tc, Uc, G, kbuf, lbuf, rbuf,
    pgl, crecv, H, zrecv, ysrc, yrecv, xbuf, res,
    local_sem, halo_send, halo_recv, core_send, core_recv, y_send, y_recv, z_send, z_recv, x_send, x_recv,
):
    ny, nz = nrow // 4, ncol // 2
    row, col = lax.axis_index("row"), lax.axis_index("col")
    y, x_lo, core = row // 4, (row // 2) % 2, row % 2
    x_hi, z = col // nz, col % nz
    x = x_hi * 2 + x_lo
    has_up, has_down = row > 0, row < nrow - 1
    has_left, has_right = col > 0, col < ncol - 1
    partner = row + 1 - 2 * core

    def y_peer(k):
        return lax.rem(y + k, ny)

    def z_peer(k):
        return lax.rem(z + k, nz)

    def x_peer(k):
        return lax.rem(x + k, 4)

    def y_id(k):
        return (y_peer(k) * 4 + x_lo * 2 + core, col)

    def z_id(k):
        return (row, x_hi * nz + z_peer(k))

    def x_id(k):
        other = x_peer(k)
        return (y * 4 + lax.rem(other, 2) * 2 + core, (other // 2) * nz + z)

    loads = [
        pltpu.make_async_copy(obj, ext.at[:, pl.ds(0, TR), pl.ds(0, TC)], local_sem.at[0]),
        pltpu.make_async_copy(probe_in, probe, local_sem.at[1]),
        pltpu.make_async_copy(inten_in, inten, local_sem.at[2]),
        pltpu.make_async_copy(tab_in, tab, local_sem.at[3]),
        pltpu.make_async_copy(row_turn_in, row_turn, local_sem.at[6]),
        pltpu.make_async_copy(lane_turn_in, lane_turn, local_sem.at[7]),
    ]
    loads[1].start()

    barrier = pltpu.get_barrier_semaphore()

    def greet(device):
        pl.semaphore_signal(barrier, inc=1, device_id=device, device_id_type=MESH)

    for k in range(1, ny):
        greet(y_id(k))
    for k in range(1, nz):
        greet(z_id(k))
    for k in range(1, 4):
        greet(x_id(k))
    far_right = has_right & (z == nz - 1)
    far_left = has_left & (z == 0)

    @pl.when(has_up)
    def _():
        greet((row - 1, col))

    @pl.when(has_down)
    def _():
        greet((row + 1, col))

    @pl.when(far_left)
    def _():
        greet((row, col - 1))

    @pl.when(far_right)
    def _():
        greet((row, col + 1))

    loads[0].start()
    loads[2].start()
    loads[3].start()
    loads[4].start()
    loads[5].start()
    one = lambda flag: flag.astype(jnp.int32)
    pl.semaphore_wait(barrier, ny + nz + 1 + one(has_up) + one(has_down) + one(far_left) + one(far_right))

    def halo(index, source, target, device):
        return pltpu.make_async_remote_copy(
            src_ref=source, dst_ref=target, send_sem=halo_send.at[index], recv_sem=halo_recv.at[index],
            device_id=device, device_id_type=MESH,
        )

    up_id = (lax.max(row - 1, 0), col)
    down_id = (lax.min(row + 1, nrow - 1), col)
    left_id = (row, lax.max(col - 1, 0))
    right_id = (row, lax.min(col + 1, ncol - 1))
    top, bottom = pl.ds(0, TR), pl.ds(TR, TR)
    main, side = pl.ds(0, TC), pl.ds(TC, N)
    half = TR // 2
    halves = (pl.ds(0, half), pl.ds(half, half))
    right_in = [
        halo(0, obj.at[:, halves[0], pl.ds(0, N)], ext.at[:, halves[0], side], left_id),
        halo(6, obj.at[:, halves[1], pl.ds(0, N)], ext.at[:, halves[1], side], left_id),
    ]
    lower_in = halo(1, obj, ext.at[:, bottom, main], up_id)
    corner_in = halo(2, ext.at[:, top, side], ext.at[:, bottom, side], up_id)

    @pl.when(has_left)
    def _():
        right_in[0].start()
        right_in[1].start()

    @pl.when(has_up)
    def _():
        lower_in.start()

    @pl.when(jnp.logical_not(has_right))
    def _():
        ext[:, :, TC:] = jnp.zeros((2, 2 * TR, N), f32)

    @pl.when(jnp.logical_not(has_down))
    def _():
        ext[:, TR:, :] = jnp.zeros((2, TR, TC + N), f32)

    @pl.when(jnp.logical_not(has_up))
    def _():
        kbuf[...] = jnp.zeros_like(kbuf)
        lbuf[...] = jnp.zeros_like(lbuf)

    @pl.when(jnp.logical_not(has_left))
    def _():
        rbuf[...] = jnp.zeros_like(rbuf)

    lanes = lax.broadcasted_iota(jnp.int32, (CH, N), 1)
    lines = lax.broadcasted_iota(jnp.int32, (CH, N), 0)

    def one_hot(flag):
        return jnp.where(flag, 1.0, 0.0).astype(bf16)

    for s in range(SLOTS):
        r = jnp.full((CH, N), offs[0, s], jnp.int32) - row * TR
        c = jnp.full((CH, N), offs[1, s], jnp.int32) - col * TC
        rvec[s] = r
        cvec[s] = c
        lvec[s] = jnp.where(jnp.full((CH, N), cnt[0], jnp.int32) > s, 1.0, 0.0)
        for b in range(3):
            cmask[s, b] = jnp.where((lanes + N * b >= c) & (lanes + N * b < c + N), 1.0, 0.0)[:8]

    def permutations(s, _):
        r, c = rvec[s], cvec[s]

        def body(i, _):
            line = lines + i * CH
            Rs[s, rows(i * CH, CH), :] = one_hot(line == ((lanes + r) & (N - 1)))
            Rt[s, rows(i * CH, CH), :] = one_hot(lanes == ((line + r) & (N - 1)))
            Cs[s, rows(i * CH, CH), :] = one_hot(lanes == ((line + c) & (N - 1)))
            Ct[s, rows(i * CH, CH), :] = one_hot(line == ((lanes + c) & (N - 1)))
            return 0

        lax.fori_loop(0, N // CH, body, 0)
        return 0

    lax.fori_loop(0, SLOTS, permutations, 0)

    loads[1].wait()

    def split_probe(i, _):
        here = rows(i * CH, CH)
        for q in range(2):
            high, low = split(probe[q, here, :])
            Pw[here, q * N:(q + 1) * N] = high
            Pw[here, (q + 2) * N:(q + 3) * N] = low
        return 0

    lax.fori_loop(0, N // CH, split_probe, 0)

    def shift_probe(s, _):
        a = dot(Rs[s], Pw[...])
        for p in range(4):
            Uc[p * N:(p + 1) * N, :] = a[:, p * N:(p + 1) * N].astype(bf16)
        a = dot(Uc[...], Cs[s])
        for q in range(2):
            Pc[s, q] = a[q * N:(q + 1) * N] + a[(q + 2) * N:(q + 3) * N]
        return 0

    lax.fori_loop(0, SLOTS, shift_probe, 0)

    loads[2].wait()
    line, lane = lax.broadcasted_iota(jnp.int32, (N, N), 0), lax.broadcasted_iota(jnp.int32, (N, N), 1)
    sort_rows = one_hot(lane == jnp.where(line < M, 2 * line, 2 * line - (N - 1)))
    sort_lanes = one_hot(line == jnp.where(lane < M, 2 * lane, 2 * lane - (N - 1)))

    def sort_intensity(s, _):
        high, low = split(inten[s])
        Uc[:N, :] = dot(sort_rows, high).astype(bf16)
        Uc[N:2 * N, :] = dot(sort_rows, low).astype(bf16)
        a = dot(Uc[:2 * N, :], sort_lanes)
        a = a[:N] + a[N:]
        Ip[s, :, :N] = a[:M]
        Ip[s, :, N:] = a[M:]
        return 0

    lax.fori_loop(0, SLOTS, sort_intensity, 0)

    @pl.when(has_right)
    def _():
        right_in[0].wait_recv()
        right_in[1].wait_recv()

        @pl.when(has_up)
        def _():
            corner_in.start()

    for load in (loads[0], loads[3], loads[4], loads[5]):
        load.wait()

    @pl.when(has_down)
    def _():
        lower_in.wait_recv()

        @pl.when(has_right)
        def _():
            corner_in.wait_recv()

    def slot(s, _):
        def gather(i, _):
            i0 = i * CH
            from_below = lines + i0 < rvec[s]
            first, second = lanes >= cvec[s], lanes + N >= cvec[s]
            parts = []
            for q in range(2):
                u = ext[q, rows(i0, CH), :]
                v = ext[q, rows(i0 + TR, CH), :]
                blocks = [jnp.where(from_below, v[:, b * N:(b + 1) * N], u[:, b * N:(b + 1) * N]) for b in range(3)]
                w = jnp.where(first, blocks[0], jnp.where(second, blocks[1], blocks[2]))
                patch[s, q, rows(i0, CH), :] = w
                parts.append(w)
            pr, pi = Pc[s, 0, rows(i0, CH), :], Pc[s, 1, rows(i0, CH), :]
            waves = (pr * parts[0] - pi * parts[1], pr * parts[1] + pi * parts[0])
            for q, wave in enumerate(waves):
                ex[s, q, rows(i0, CH), :] = wave
            turn = (lane_turn[0, rows(i0, CH), :], lane_turn[1, rows(i0, CH), :])
            pair = forward_half([w[:, :M] for w in waves], [w[:, M:] for w in waves], *turn)
            for b in range(2):
                for q in range(2):
                    high, low = split(pair[b][q])
                    X[s, rows(i0 + b * N, CH), q * M:(q + 1) * M] = high
                    X[s, rows(i0 + (b + 2) * N, CH), q * M:(q + 1) * M] = low
            return 0

        lax.fori_loop(0, N // CH, gather, 0, unroll=8)
        a = dot(X[s], tab[0, 0])
        a = a[:2 * N] + a[2 * N:] + dot(X[s, :2 * N], tab[0, 1])
        a = [jnp.concatenate([a[:N, q * M:(q + 1) * M], a[N:, q * M:(q + 1) * M]], axis=1) for q in range(2)]
        pair = forward_half([w[:M] for w in a], [w[M:] for w in a], row_turn[0], row_turn[1])
        for b in range(2):
            for q in range(2):
                high, low = split(pair[b][q])
                Y[s, q * M:(q + 1) * M, b * N:(b + 1) * N] = high
                Y[s, q * M:(q + 1) * M, (b + 2) * N:(b + 3) * N] = low
        a = dot(tab[1, 0], Y[s])
        D[s] = a[:, :2 * N] + a[:, 2 * N:] + dot(tab[1, 1], Y[s, :, :2 * N])

        def project(i, _):
            i0 = i * 16
            zr, zi = D[s, rows(i0, 16), :], D[s, rows(i0 + M, 16), :]
            measured = Ip[s, rows(i0, 16), :]
            factor = measured * lax.rsqrt(measured * (zr * zr + zi * zi + stabilizer))
            for q, wave in enumerate((zr * factor, zi * factor)):
                high, low = split(wave)
                there = pl.ds(pl.multiple_of(i0 + q * M, 16), 16)
                Pj[s, there, :2 * N] = high
                Pj[s, there, 2 * N:] = low
            return 0

        lax.fori_loop(0, M // 16, project, 0, unroll=8)
        a = dot(tab[0, 0], Pj[s])
        a = a[:, :2 * N] + a[:, 2 * N:] + dot(tab[0, 1], Pj[s, :, :2 * N])
        pair = backward_half((a[:M, :N], a[M:, :N]), (a[:M, N:], a[M:, N:]), row_turn[0], row_turn[1])
        for b in range(2):
            for q in range(2):
                high, low = split(pair[b][q])
                for part in range(2):
                    there = slice(part * N + b * M, part * N + (b + 1) * M)
                    below = slice((part + 2) * N + b * M, (part + 2) * N + (b + 1) * M)
                    X[s, there, q * M:(q + 1) * M] = high[:, part * M:(part + 1) * M]
                    X[s, below, q * M:(q + 1) * M] = low[:, part * M:(part + 1) * M]
        a = dot(X[s], tab[1, 0])
        a = a[:2 * N] + a[2 * N:] + dot(X[s, :2 * N], tab[1, 1])
        pair = backward_half((a[:N, :M], a[:N, M:]), (a[N:, :M], a[N:, M:]), lane_turn[0], lane_turn[1])
        for b in range(2):
            for q in range(2):
                B[q * N:(q + 1) * N, b * M:(b + 1) * M] = pair[b][q]

        def finish(i, _):
            i0 = i * CH
            here, below = rows(i0, CH), rows(i0 + N, CH)
            live = lvec[s]
            dr = (ex[s, 0, here, :] - B[here, :]) * live
            di = (ex[s, 1, here, :] - B[below, :]) * live
            wr, wi = patch[s, 0, here, :], patch[s, 1, here, :]
            for q, term in enumerate((wr * dr + wi * di, wr * di - wi * dr)):
                high, low = split(term)
                Tc[here, q * N:(q + 1) * N] = high
                Tc[here, (q + 2) * N:(q + 3) * N] = low
            pr, pi = Pc[s, 0, here, :], Pc[s, 1, here, :]
            ex[s, 0, here, :] = pr * dr + pi * di
            ex[s, 1, here, :] = pr * di - pi * dr
            return 0

        lax.fori_loop(0, N // CH, finish, 0, unroll=8)

        a = dot(Rt[s], Tc[...])
        for q in range(2):
            high, low = split(a[:, q * N:(q + 1) * N] + a[:, (q + 2) * N:(q + 3) * N])
            Uc[q * N:(q + 1) * N, :] = high
            Uc[(q + 2) * N:(q + 3) * N, :] = low
        a = dot(Uc[...], Ct[s])
        for q in range(2):
            pgl[q] += a[q * N:(q + 1) * N] + a[(q + 2) * N:(q + 3) * N]
        return 0

    pgl[...] = jnp.zeros_like(pgl)
    lax.fori_loop(0, SLOTS, slot, 0)

    def remote(source, target, send, recv, device):
        return pltpu.make_async_remote_copy(
            src_ref=source, dst_ref=target, send_sem=send, recv_sem=recv, device_id=device, device_id_type=MESH
        )

    to_partner = remote(pgl.at[1 - core], crecv, core_send.at[0], core_recv.at[0], (partner, col))
    to_partner.start()

    def deposit(i, _):
        i0 = i * 8
        here, below = rows(i0, 8), rows(i0 + N, 8)
        for q in range(2):
            terms = [ex[s, q, here, :] for s in range(SLOTS)]
            lower = [jnp.where(lines[:8] + i0 < rvec[s, :8], terms[s], 0.0) for s in range(SLOTS)]
            upper = [terms[s] - lower[s] for s in range(SLOTS)]
            for b in range(3):
                for part, target in ((lower, below), (upper, here)):
                    kept = [part[s] * cmask[s, b] for s in range(SLOTS)]
                    G[q, target, b * N:(b + 1) * N] = (kept[0] + kept[1]) + (kept[2] + kept[3])
        return 0

    lax.fori_loop(0, N // 8, deposit, 0, unroll=4)

    corner_out = halo(3, G.at[:, bottom, side], kbuf, down_id)
    lower_out = halo(4, G.at[:, bottom, main], lbuf, down_id)
    right_out = [
        halo(5, G.at[:, halves[0], side], rbuf.at[:, halves[0], :], right_id),
        halo(8, G.at[:, halves[1], side], rbuf.at[:, halves[1], :], right_id),
    ]

    @pl.when(has_down)
    def _():
        corner_out.start()
        lower_out.start()

    to_partner.wait_recv()

    def add_core(i, _):
        for p in range(nz):
            here = rows(i * nz * 8 + p * 8, 8)
            H[i, p] = pgl[core, here, :] + crecv[here, :]
        return 0

    lax.fori_loop(0, N // (8 * nz), add_core, 0, unroll=True)
    z_out = [remote(H.at[:, z_peer(k)], zrecv.at[k], z_send.at[k], z_recv.at[k], z_id(k)) for k in range(1, nz)]
    for copy in z_out:
        copy.start()

    for copy in z_out:
        copy.wait_recv()
    for a in range(N // (8 * nz)):
        summed = H[a, z]
        for k in range(1, nz):
            summed = summed + zrecv[k, a]
        for half in range(2):
            ysrc[2 * a + half] = summed[:, 128 * half:128 * half + 128]
    y_out = [remote(ysrc.at[y_peer(k)], yrecv.at[k], y_send.at[k], y_recv.at[k], y_id(k)) for k in range(1, ny)]
    for copy in y_out:
        copy.start()
    @pl.when(has_up)
    def _():
        corner_out.wait_recv()

    def add_corner(i, _):
        for q in range(2):
            G[q, rows(i * CH, CH), TC:] += kbuf[q, rows(i * CH, CH), :]
        return 0

    lax.fori_loop(0, TR // CH, add_corner, 0, unroll=8)

    @pl.when(has_right)
    def _():
        right_out[0].start()
        right_out[1].start()

    for copy in y_out:
        copy.wait_recv()
    tile = ysrc[y]
    for k in range(1, ny):
        tile = tile + yrecv[k]
    xbuf[x] = tile
    x_out = [remote(xbuf.at[x], xbuf.at[x], x_send.at[k], x_recv.at[k], x_id(k)) for k in range(1, 4)]
    for copy in x_out:
        copy.start()
    for copy in x_out:
        copy.wait_recv()
    tile = ((xbuf[0] + xbuf[1]) + (xbuf[2] + xbuf[3])) * f32(1.0 / math.sqrt(SLOTS * nrow * ncol))
    my_lanes = pl.ds(pl.multiple_of(128 * (y % 2), 128), 128)
    my_tile = (core, rows(8 * nz * (y // 2) + 8 * z, 8), my_lanes)
    res[my_tile] = tile
    z_back = [remote(res.at[my_tile], res.at[my_tile], z_send.at[nz + k], z_recv.at[nz + k], z_id(k)) for k in range(1, nz)]
    for copy in z_back:
        copy.start()

    for copy in z_back:
        copy.wait_recv()
    my_rows = (core, rows(8 * nz * (y // 2), 8 * nz), my_lanes)
    y_back = [remote(res.at[my_rows], res.at[my_rows], y_send.at[ny + k], y_recv.at[ny + k], y_id(k)) for k in range(1, ny)]
    for copy in y_back:
        copy.start()
    for copy in y_back:
        copy.wait_recv()
    share = remote(res.at[core], res.at[core], core_send.at[1], core_recv.at[1], (partner, col))
    share.start()

    @pl.when(has_up)
    def _():
        lower_out.wait_recv()

    @pl.when(has_left)
    def _():
        right_out[0].wait_recv()
        right_out[1].wait_recv()

    def add_halos(i, _):
        here = rows(i * CH, CH)
        for q in range(2):
            G[q, here, :N] = G[q, here, :N] + lbuf[q, here, :N] + rbuf[q, here, :]
            G[q, here, N:TC] = G[q, here, N:TC] + lbuf[q, here, N:]
        return 0

    lax.fori_loop(0, TR // CH, add_halos, 0, unroll=8)
    store_grad = pltpu.make_async_copy(G.at[:, top, main], grad_out, local_sem.at[4])
    store_grad.start()
    share.wait_recv()
    store_probe = pltpu.make_async_copy(res, pg_out, local_sem.at[5])
    store_probe.start()

    @pl.when(has_left)
    def _():
        right_in[0].wait_send()
        right_in[1].wait_send()

    @pl.when(has_up)
    def _():
        lower_in.wait_send()

        @pl.when(has_right)
        def _():
            corner_in.wait_send()

    @pl.when(has_down)
    def _():
        corner_out.wait_send()
        lower_out.wait_send()

    @pl.when(has_right)
    def _():
        right_out[0].wait_send()
        right_out[1].wait_send()

    to_partner.wait_send()
    share.wait_send()
    for copy in y_out + z_out + x_out + z_back + y_back:
        copy.wait_send()
    store_grad.wait()
    store_probe.wait()


def local(nrow, ncol, object_field, probe_field, intensity, offsets, counts):
    ny, nz = nrow // 4, ncol // 2
    anywhere = pl.BlockSpec(memory_space=pl.ANY)
    scalars = pl.BlockSpec(memory_space=pltpu.SMEM)
    vmem = pltpu.VMEM
    dma = pltpu.SemaphoreType.DMA
    grad, probe_grad = pl.pallas_call(
        functools.partial(kernel, nrow, ncol),
        out_shape=[jax.ShapeDtypeStruct((2, TR, TC), f32), jax.ShapeDtypeStruct((2, N, N), f32)],
        in_specs=[scalars, scalars] + [anywhere] * 6,
        out_specs=[anywhere, anywhere],
        scratch_shapes=[
            vmem((2, 2 * TR, TC + N), f32),
            vmem((2, N, N), f32),
            vmem((SLOTS, N, N), f32),
            vmem((2, 2, N, N), bf16),
            vmem((2, M, N), f32),
            vmem((2, N, M), f32),
            vmem((SLOTS, M, 2 * N), f32),
            vmem((SLOTS, N, N), bf16),
            vmem((SLOTS, N, N), bf16),
            vmem((SLOTS, N, N), bf16),
            vmem((SLOTS, N, N), bf16),
            vmem((SLOTS, CH, N), jnp.int32),
            vmem((SLOTS, CH, N), jnp.int32),
            vmem((SLOTS, CH, N), f32),
            vmem((SLOTS, 3, 8, N), f32),
            vmem((N, 4 * N), bf16),
            vmem((SLOTS, 2, N, N), f32),
            vmem((SLOTS, 4 * N, N), bf16),
            vmem((SLOTS, N, 4 * N), bf16),
            vmem((SLOTS, N, 4 * N), bf16),
            vmem((SLOTS, N, 2 * N), f32),
            vmem((2 * N, N), f32),
            vmem((SLOTS, 2, N, N), f32),
            vmem((SLOTS, 2, N, N), f32),
            vmem((N, 4 * N), bf16),
            vmem((4 * N, N), bf16),
            vmem((2, 2 * TR, TC + N), f32),
            vmem((2, TR, N), f32),
            vmem((2, TR, TC), f32),
            vmem((2, TR, N), f32),
            vmem((2, N, N), f32),
            vmem((N, N), f32),
            vmem((N // (8 * nz), nz, 8, N), f32),
            vmem((nz, N // (8 * nz), 8, N), f32),
            vmem((ny, 8, 128), f32),
            vmem((ny, 8, 128), f32),
            vmem((4, 8, 128), f32),
            vmem((2, N, N), f32),
            dma((8,)), dma((9,)), dma((9,)), dma((2,)), dma((2,)),
            dma((2 * ny,)), dma((2 * ny,)), dma((2 * nz,)), dma((2 * nz,)), dma((4,)), dma((4,)),
        ],
        compiler_params=pltpu.CompilerParams(collective_id=0, has_side_effects=True, vmem_limit_bytes=56 * 2**20),
    )(offsets.T, counts, object_field, probe_field, intensity, jnp.asarray(dft_tables()), *(jnp.asarray(t) for t in twiddles()))
    return grad, probe_grad


def solution(mesh):
    in_specs = (
        P(None, "row", "col"),
        P(),
        P(("row", "col"), None, None),
        P(("row", "col"), None),
        P(("row", "col")),
    )
    out_specs = (P(None, "row", "col"), P())
    body = functools.partial(local, mesh.shape["row"], mesh.shape["col"])
    return jax.shard_map(body, mesh=mesh, in_specs=in_specs, out_specs=out_specs, check_vma=False)
```

```python
import functools
import math

import jax
import jax.numpy as jnp
import ml_dtypes
import numpy as np
from jax import lax
from jax.experimental import pallas as pl
from jax.experimental.pallas import tpu as pltpu
from jax.sharding import PartitionSpec as P

MESH = pl.DeviceIdType.MESH
f32 = jnp.float32
bf16 = jnp.bfloat16
stabilizer = 0.01
N = 256
TR = 256
TC = 512
SLOTS = 4
CH = 32
M = N // 2
PARTS = 4


def dft_tables():
    index = np.arange(M)
    angles = (index[:, None] * index[None, :] % M) * (2.0 * np.pi / M)
    c = np.cos(angles) / math.sqrt(N)
    s = np.sin(angles) / math.sqrt(N)
    both = np.stack([np.block([[c, -s], [s, c]]), np.block([[c, s], [-s, c]])]).astype(np.float32)
    high = both.astype(ml_dtypes.bfloat16)
    low = (both - high.astype(np.float32)).astype(ml_dtypes.bfloat16)
    return np.stack([high, low], axis=1)


def twiddles():
    angles = np.arange(M) * (2.0 * np.pi / N)
    pair = np.stack([np.cos(angles), np.sin(angles)]).astype(np.float32)
    return np.broadcast_to(pair[:, :, None], (2, M, N)).copy(), np.broadcast_to(pair[:, None, :], (2, N, M)).copy()


def rows(start, size):
    return pl.ds(pl.multiple_of(start, 8), size)


def split(value):
    high = value.astype(bf16)
    return high, (value - high.astype(f32)).astype(bf16)


def dot(a, b):
    return jnp.dot(a, b, preferred_element_type=f32)


def forward_half(tops, bottoms, cosine, sine):
    real, imag = tops[0] - bottoms[0], tops[1] - bottoms[1]
    odd = (real * cosine + imag * sine, imag * cosine - real * sine)
    return (tops[0] + bottoms[0], tops[1] + bottoms[1]), odd


def backward_half(even, odd, cosine, sine):
    real, imag = odd[0] * cosine - odd[1] * sine, odd[0] * sine + odd[1] * cosine
    return (even[0] + real, even[1] + imag), (even[0] - real, even[1] - imag)


def kernel(
    nrow, ncol,
    offs, cnt, obj, probe_in, inten_in, tab_in, row_turn_in, lane_turn_in,
    grad_out, pg_out,
    ext, probe, inten, tab, row_turn, lane_turn, Ip, Rs, Rt, Cs, Ct, rvec, cvec, lvec, cmask, Pw, Pc, X, Y, Pj, D, B, patch, ex, Tc, Uc, G, kbuf, lbuf, rbuf,
    pgl, crecv, H, zrecv, ysrc, yrecv, xbuf, res,
    local_sem, halo_send, halo_recv, core_send, core_recv, y_send, y_recv, z_send, z_recv, x_send, x_recv,
):
    ny, nz = nrow // 4, ncol // 2
    row, col = lax.axis_index("row"), lax.axis_index("col")
    y, x_lo, core = row // 4, (row // 2) % 2, row % 2
    x_hi, z = col // nz, col % nz
    x = x_hi * 2 + x_lo
    has_up, has_down = row > 0, row < nrow - 1
    has_left, has_right = col > 0, col < ncol - 1
    partner = row + 1 - 2 * core

    def y_peer(k):
        return lax.rem(y + k, ny)

    def z_peer(k):
        return lax.rem(z + k, nz)

    def x_peer(k):
        return lax.rem(x + k, 4)

    def y_id(k):
        return (y_peer(k) * 4 + x_lo * 2 + core, col)

    def z_id(k):
        return (row, x_hi * nz + z_peer(k))

    def x_id(k):
        other = x_peer(k)
        return (y * 4 + lax.rem(other, 2) * 2 + core, (other // 2) * nz + z)

    loads = [
        pltpu.make_async_copy(obj, ext.at[:, pl.ds(0, TR), pl.ds(0, TC)], local_sem.at[0]),
        pltpu.make_async_copy(probe_in, probe, local_sem.at[1]),
        pltpu.make_async_copy(inten_in, inten, local_sem.at[2]),
        pltpu.make_async_copy(tab_in, tab, local_sem.at[3]),
        pltpu.make_async_copy(row_turn_in, row_turn, local_sem.at[6]),
        pltpu.make_async_copy(lane_turn_in, lane_turn, local_sem.at[7]),
    ]
    loads[1].start()

    barrier = pltpu.get_barrier_semaphore()

    def greet(device):
        pl.semaphore_signal(barrier, inc=1, device_id=device, device_id_type=MESH)

    for k in range(1, ny):
        greet(y_id(k))
    for k in range(1, nz):
        greet(z_id(k))
    for k in range(1, 4):
        greet(x_id(k))
    far_right = has_right & (z == nz - 1)
    far_left = has_left & (z == 0)

    @pl.when(has_up)
    def _():
        greet((row - 1, col))

    @pl.when(has_down)
    def _():
        greet((row + 1, col))

    @pl.when(far_left)
    def _():
        greet((row, col - 1))

    @pl.when(far_right)
    def _():
        greet((row, col + 1))

    loads[0].start()
    loads[2].start()
    loads[3].start()
    loads[4].start()
    loads[5].start()
    one = lambda flag: flag.astype(jnp.int32)
    pl.semaphore_wait(barrier, ny + nz + 1 + one(has_up) + one(has_down) + one(far_left) + one(far_right))

    def halo(index, source, target, device):
        return pltpu.make_async_remote_copy(
            src_ref=source, dst_ref=target, send_sem=halo_send.at[index], recv_sem=halo_recv.at[index],
            device_id=device, device_id_type=MESH,
        )

    up_id = (lax.max(row - 1, 0), col)
    down_id = (lax.min(row + 1, nrow - 1), col)
    left_id = (row, lax.max(col - 1, 0))
    right_id = (row, lax.min(col + 1, ncol - 1))
    top, bottom = pl.ds(0, TR), pl.ds(TR, TR)
    main, side = pl.ds(0, TC), pl.ds(TC, N)
    step = TR // PARTS
    strips = [pl.ds(b * step, step) for b in range(PARTS)]
    lower_strips = [pl.ds(TR + b * step, step) for b in range(PARTS)]
    right_in = [
        halo(2 + b, obj.at[:, strips[b], pl.ds(0, N)], ext.at[:, strips[b], side], left_id) for b in range(PARTS)
    ]
    corner_in = [
        halo(2 + PARTS + b, ext.at[:, strips[b], side], ext.at[:, lower_strips[b], side], up_id) for b in range(PARTS)
    ]
    lower_in = halo(0, obj, ext.at[:, bottom, main], up_id)

    @pl.when(has_left)
    def _():
        for copy in right_in:
            copy.start()

    @pl.when(has_up)
    def _():
        lower_in.start()

    @pl.when(jnp.logical_not(has_right))
    def _():
        ext[:, :, TC:] = jnp.zeros((2, 2 * TR, N), f32)

    @pl.when(jnp.logical_not(has_down))
    def _():
        ext[:, TR:, :] = jnp.zeros((2, TR, TC + N), f32)

    @pl.when(jnp.logical_not(has_up))
    def _():
        kbuf[...] = jnp.zeros_like(kbuf)
        lbuf[...] = jnp.zeros_like(lbuf)

    @pl.when(jnp.logical_not(has_left))
    def _():
        rbuf[...] = jnp.zeros_like(rbuf)

    lanes = lax.broadcasted_iota(jnp.int32, (CH, N), 1)
    lines = lax.broadcasted_iota(jnp.int32, (CH, N), 0)

    def one_hot(flag):
        return jnp.where(flag, 1.0, 0.0).astype(bf16)

    for s in range(SLOTS):
        r = jnp.full((CH, N), offs[0, s], jnp.int32) - row * TR
        c = jnp.full((CH, N), offs[1, s], jnp.int32) - col * TC
        rvec[s] = r
        cvec[s] = c
        lvec[s] = jnp.where(jnp.full((CH, N), cnt[0], jnp.int32) > s, 1.0, 0.0)
        for b in range(3):
            cmask[s, b] = jnp.where((lanes + N * b >= c) & (lanes + N * b < c + N), 1.0, 0.0)[:8]

    def permutations(s, _):
        r, c = rvec[s], cvec[s]

        def body(i, _):
            line = lines + i * CH
            Rs[s, rows(i * CH, CH), :] = one_hot(line == ((lanes + r) & (N - 1)))
            Rt[s, rows(i * CH, CH), :] = one_hot(lanes == ((line + r) & (N - 1)))
            Cs[s, rows(i * CH, CH), :] = one_hot(lanes == ((line + c) & (N - 1)))
            Ct[s, rows(i * CH, CH), :] = one_hot(line == ((lanes + c) & (N - 1)))
            return 0

        lax.fori_loop(0, N // CH, body, 0)
        return 0

    lax.fori_loop(0, SLOTS, permutations, 0)

    loads[1].wait()

    def split_probe(i, _):
        here = rows(i * CH, CH)
        for q in range(2):
            high, low = split(probe[q, here, :])
            Pw[here, q * N:(q + 1) * N] = high
            Pw[here, (q + 2) * N:(q + 3) * N] = low
        return 0

    lax.fori_loop(0, N // CH, split_probe, 0)

    def shift_probe(s, _):
        a = dot(Rs[s], Pw[...])
        for p in range(4):
            Uc[p * N:(p + 1) * N, :] = a[:, p * N:(p + 1) * N].astype(bf16)
        a = dot(Uc[...], Cs[s])
        for q in range(2):
            Pc[s, q] = a[q * N:(q + 1) * N] + a[(q + 2) * N:(q + 3) * N]
        return 0

    lax.fori_loop(0, SLOTS, shift_probe, 0)

    loads[2].wait()
    line, lane = lax.broadcasted_iota(jnp.int32, (N, N), 0), lax.broadcasted_iota(jnp.int32, (N, N), 1)
    sort_rows = one_hot(lane == jnp.where(line < M, 2 * line, 2 * line - (N - 1)))
    sort_lanes = one_hot(line == jnp.where(lane < M, 2 * lane, 2 * lane - (N - 1)))

    def sort_intensity(s, _):
        high, low = split(inten[s])
        Uc[:N, :] = dot(sort_rows, high).astype(bf16)
        Uc[N:2 * N, :] = dot(sort_rows, low).astype(bf16)
        a = dot(Uc[:2 * N, :], sort_lanes)
        a = a[:N] + a[N:]
        Ip[s, :, :N] = a[:M]
        Ip[s, :, N:] = a[M:]
        return 0

    lax.fori_loop(0, SLOTS, sort_intensity, 0)

    @pl.when(has_right)
    def _():
        for b in range(PARTS):
            right_in[b].wait_recv()

            @pl.when(has_up)
            def _():
                corner_in[b].start()

    for load in (loads[0], loads[3], loads[4], loads[5]):
        load.wait()

    @pl.when(has_down)
    def _():
        lower_in.wait_recv()

        @pl.when(has_right)
        def _():
            for copy in corner_in:
                copy.wait_recv()

    def slot(s, _):
        def gather(i, _):
            i0 = i * CH
            from_below = lines + i0 < rvec[s]
            first, second = lanes >= cvec[s], lanes + N >= cvec[s]
            parts = []
            for q in range(2):
                u = ext[q, rows(i0, CH), :]
                v = ext[q, rows(i0 + TR, CH), :]
                blocks = [jnp.where(from_below, v[:, b * N:(b + 1) * N], u[:, b * N:(b + 1) * N]) for b in range(3)]
                w = jnp.where(first, blocks[0], jnp.where(second, blocks[1], blocks[2]))
                patch[s, q, rows(i0, CH), :] = w
                parts.append(w)
            pr, pi = Pc[s, 0, rows(i0, CH), :], Pc[s, 1, rows(i0, CH), :]
            waves = (pr * parts[0] - pi * parts[1], pr * parts[1] + pi * parts[0])
            for q, wave in enumerate(waves):
                ex[s, q, rows(i0, CH), :] = wave
            turn = (lane_turn[0, rows(i0, CH), :], lane_turn[1, rows(i0, CH), :])
            pair = forward_half([w[:, :M] for w in waves], [w[:, M:] for w in waves], *turn)
            for b in range(2):
                for q in range(2):
                    high, low = split(pair[b][q])
                    X[s, rows(i0 + b * N, CH), q * M:(q + 1) * M] = high
                    X[s, rows(i0 + (b + 2) * N, CH), q * M:(q + 1) * M] = low
            return 0

        lax.fori_loop(0, N // CH, gather, 0, unroll=8)
        a = dot(X[s], tab[0, 0])
        a = a[:2 * N] + a[2 * N:] + dot(X[s, :2 * N], tab[0, 1])
        a = [jnp.concatenate([a[:N, q * M:(q + 1) * M], a[N:, q * M:(q + 1) * M]], axis=1) for q in range(2)]
        pair = forward_half([w[:M] for w in a], [w[M:] for w in a], row_turn[0], row_turn[1])
        for b in range(2):
            for q in range(2):
                high, low = split(pair[b][q])
                Y[s, q * M:(q + 1) * M, b * N:(b + 1) * N] = high
                Y[s, q * M:(q + 1) * M, (b + 2) * N:(b + 3) * N] = low
        a = dot(tab[1, 0], Y[s])
        D[s] = a[:, :2 * N] + a[:, 2 * N:] + dot(tab[1, 1], Y[s, :, :2 * N])

        def project(i, _):
            i0 = i * 16
            zr, zi = D[s, rows(i0, 16), :], D[s, rows(i0 + M, 16), :]
            measured = Ip[s, rows(i0, 16), :]
            factor = measured * lax.rsqrt(measured * (zr * zr + zi * zi + stabilizer))
            for q, wave in enumerate((zr * factor, zi * factor)):
                high, low = split(wave)
                there = pl.ds(pl.multiple_of(i0 + q * M, 16), 16)
                Pj[s, there, :2 * N] = high
                Pj[s, there, 2 * N:] = low
            return 0

        lax.fori_loop(0, M // 16, project, 0, unroll=8)
        a = dot(tab[0, 0], Pj[s])
        a = a[:, :2 * N] + a[:, 2 * N:] + dot(tab[0, 1], Pj[s, :, :2 * N])
        pair = backward_half((a[:M, :N], a[M:, :N]), (a[:M, N:], a[M:, N:]), row_turn[0], row_turn[1])
        for b in range(2):
            for q in range(2):
                high, low = split(pair[b][q])
                for part in range(2):
                    there = slice(part * N + b * M, part * N + (b + 1) * M)
                    below = slice((part + 2) * N + b * M, (part + 2) * N + (b + 1) * M)
                    X[s, there, q * M:(q + 1) * M] = high[:, part * M:(part + 1) * M]
                    X[s, below, q * M:(q + 1) * M] = low[:, part * M:(part + 1) * M]
        a = dot(X[s], tab[1, 0])
        a = a[:2 * N] + a[2 * N:] + dot(X[s, :2 * N], tab[1, 1])
        pair = backward_half((a[:N, :M], a[:N, M:]), (a[N:, :M], a[N:, M:]), lane_turn[0], lane_turn[1])
        for b in range(2):
            for q in range(2):
                B[q * N:(q + 1) * N, b * M:(b + 1) * M] = pair[b][q]

        def finish(i, _):
            i0 = i * CH
            here, below = rows(i0, CH), rows(i0 + N, CH)
            live = lvec[s]
            dr = (ex[s, 0, here, :] - B[here, :]) * live
            di = (ex[s, 1, here, :] - B[below, :]) * live
            wr, wi = patch[s, 0, here, :], patch[s, 1, here, :]
            for q, term in enumerate((wr * dr + wi * di, wr * di - wi * dr)):
                high, low = split(term)
                Tc[here, q * N:(q + 1) * N] = high
                Tc[here, (q + 2) * N:(q + 3) * N] = low
            pr, pi = Pc[s, 0, here, :], Pc[s, 1, here, :]
            ex[s, 0, here, :] = pr * dr + pi * di
            ex[s, 1, here, :] = pr * di - pi * dr
            return 0

        lax.fori_loop(0, N // CH, finish, 0, unroll=8)

        a = dot(Rt[s], Tc[...])
        for q in range(2):
            high, low = split(a[:, q * N:(q + 1) * N] + a[:, (q + 2) * N:(q + 3) * N])
            Uc[q * N:(q + 1) * N, :] = high
            Uc[(q + 2) * N:(q + 3) * N, :] = low
        a = dot(Uc[...], Ct[s])
        for q in range(2):
            pgl[q] += a[q * N:(q + 1) * N] + a[(q + 2) * N:(q + 3) * N]
        return 0

    pgl[...] = jnp.zeros_like(pgl)
    lax.fori_loop(0, SLOTS, slot, 0, unroll=2)

    def remote(source, target, send, recv, device):
        return pltpu.make_async_remote_copy(
            src_ref=source, dst_ref=target, send_sem=send, recv_sem=recv, device_id=device, device_id_type=MESH
        )

    to_partner = remote(pgl.at[1 - core], crecv, core_send.at[0], core_recv.at[0], (partner, col))
    to_partner.start()

    def deposit(i, _):
        i0 = i * 8
        here, below = rows(i0, 8), rows(i0 + N, 8)
        for q in range(2):
            terms = [ex[s, q, here, :] for s in range(SLOTS)]
            lower = [jnp.where(lines[:8] + i0 < rvec[s, :8], terms[s], 0.0) for s in range(SLOTS)]
            upper = [terms[s] - lower[s] for s in range(SLOTS)]
            for b in range(3):
                for part, target in ((lower, below), (upper, here)):
                    kept = [part[s] * cmask[s, b] for s in range(SLOTS)]
                    G[q, target, b * N:(b + 1) * N] = (kept[0] + kept[1]) + (kept[2] + kept[3])
        return 0

    lax.fori_loop(0, N // 8, deposit, 0, unroll=4)

    corner_out = [
        halo(2 + 2 * PARTS + b, G.at[:, lower_strips[b], side], kbuf.at[:, strips[b], :], down_id) for b in range(PARTS)
    ]
    right_out = [
        halo(2 + 3 * PARTS + b, G.at[:, strips[b], side], rbuf.at[:, strips[b], :], right_id) for b in range(PARTS)
    ]
    lower_out = halo(1, G.at[:, bottom, main], lbuf, down_id)

    @pl.when(has_down)
    def _():
        for copy in corner_out:
            copy.start()
        lower_out.start()

    to_partner.wait_recv()

    def add_core(i, _):
        for p in range(nz):
            here = rows(i * nz * 8 + p * 8, 8)
            H[i, p] = pgl[core, here, :] + crecv[here, :]
        return 0

    lax.fori_loop(0, N // (8 * nz), add_core, 0, unroll=True)
    z_out = [remote(H.at[:, z_peer(k)], zrecv.at[k], z_send.at[k], z_recv.at[k], z_id(k)) for k in range(1, nz)]
    for copy in z_out:
        copy.start()

    for copy in z_out:
        copy.wait_recv()
    for a in range(N // (8 * nz)):
        summed = H[a, z]
        for k in range(1, nz):
            summed = summed + zrecv[k, a]
        for half in range(2):
            ysrc[2 * a + half] = summed[:, 128 * half:128 * half + 128]
    y_out = [remote(ysrc.at[y_peer(k)], yrecv.at[k], y_send.at[k], y_recv.at[k], y_id(k)) for k in range(1, ny)]
    for copy in y_out:
        copy.start()
    def add_corner(i, _):
        for q in range(2):
            G[q, rows(i * CH, CH), TC:] += kbuf[q, rows(i * CH, CH), :]
        return 0

    def pass_corner(b):
        @pl.when(has_up)
        def _():
            corner_out[b].wait_recv()

        lax.fori_loop(b * step // CH, (b + 1) * step // CH, add_corner, 0, unroll=True)

        @pl.when(has_right)
        def _():
            right_out[b].start()

    for b in range(PARTS):
        pass_corner(b)

    for copy in y_out:
        copy.wait_recv()
    tile = ysrc[y]
    for k in range(1, ny):
        tile = tile + yrecv[k]
    xbuf[x] = tile
    x_out = [remote(xbuf.at[x], xbuf.at[x], x_send.at[k], x_recv.at[k], x_id(k)) for k in range(1, 4)]
    for copy in x_out:
        copy.start()
    for copy in x_out:
        copy.wait_recv()
    tile = ((xbuf[0] + xbuf[1]) + (xbuf[2] + xbuf[3])) * f32(1.0 / math.sqrt(SLOTS * nrow * ncol))
    my_lanes = pl.ds(pl.multiple_of(128 * (y % 2), 128), 128)
    my_tile = (core, rows(8 * nz * (y // 2) + 8 * z, 8), my_lanes)
    res[my_tile] = tile
    z_back = [remote(res.at[my_tile], res.at[my_tile], z_send.at[nz + k], z_recv.at[nz + k], z_id(k)) for k in range(1, nz)]
    for copy in z_back:
        copy.start()

    for copy in z_back:
        copy.wait_recv()
    my_rows = (core, rows(8 * nz * (y // 2), 8 * nz), my_lanes)
    y_back = [remote(res.at[my_rows], res.at[my_rows], y_send.at[ny + k], y_recv.at[ny + k], y_id(k)) for k in range(1, ny)]
    for copy in y_back:
        copy.start()
    for copy in y_back:
        copy.wait_recv()
    share = remote(res.at[core], res.at[core], core_send.at[1], core_recv.at[1], (partner, col))
    share.start()

    @pl.when(has_up)
    def _():
        lower_out.wait_recv()

    @pl.when(has_left)
    def _():
        for copy in right_out:
            copy.wait_recv()

    def add_halos(i, _):
        here = rows(i * CH, CH)
        for q in range(2):
            G[q, here, :N] = G[q, here, :N] + lbuf[q, here, :N] + rbuf[q, here, :]
            G[q, here, N:TC] = G[q, here, N:TC] + lbuf[q, here, N:]
        return 0

    lax.fori_loop(0, TR // CH, add_halos, 0, unroll=8)
    store_grad = pltpu.make_async_copy(G.at[:, top, main], grad_out, local_sem.at[4])
    store_grad.start()
    share.wait_recv()
    store_probe = pltpu.make_async_copy(res, pg_out, local_sem.at[5])
    store_probe.start()

    @pl.when(has_left)
    def _():
        for copy in right_in:
            copy.wait_send()

    @pl.when(has_up)
    def _():
        lower_in.wait_send()

        @pl.when(has_right)
        def _():
            for copy in corner_in:
                copy.wait_send()

    @pl.when(has_down)
    def _():
        for copy in corner_out:
            copy.wait_send()
        lower_out.wait_send()

    @pl.when(has_right)
    def _():
        for copy in right_out:
            copy.wait_send()

    to_partner.wait_send()
    share.wait_send()
    for copy in y_out + z_out + x_out + z_back + y_back:
        copy.wait_send()
    store_grad.wait()
    store_probe.wait()


def local(nrow, ncol, object_field, probe_field, intensity, offsets, counts):
    ny, nz = nrow // 4, ncol // 2
    anywhere = pl.BlockSpec(memory_space=pl.ANY)
    scalars = pl.BlockSpec(memory_space=pltpu.SMEM)
    vmem = pltpu.VMEM
    dma = pltpu.SemaphoreType.DMA
    grad, probe_grad = pl.pallas_call(
        functools.partial(kernel, nrow, ncol),
        out_shape=[jax.ShapeDtypeStruct((2, TR, TC), f32), jax.ShapeDtypeStruct((2, N, N), f32)],
        in_specs=[scalars, scalars] + [anywhere] * 6,
        out_specs=[anywhere, anywhere],
        scratch_shapes=[
            vmem((2, 2 * TR, TC + N), f32),
            vmem((2, N, N), f32),
            vmem((SLOTS, N, N), f32),
            vmem((2, 2, N, N), bf16),
            vmem((2, M, N), f32),
            vmem((2, N, M), f32),
            vmem((SLOTS, M, 2 * N), f32),
            vmem((SLOTS, N, N), bf16),
            vmem((SLOTS, N, N), bf16),
            vmem((SLOTS, N, N), bf16),
            vmem((SLOTS, N, N), bf16),
            vmem((SLOTS, CH, N), jnp.int32),
            vmem((SLOTS, CH, N), jnp.int32),
            vmem((SLOTS, CH, N), f32),
            vmem((SLOTS, 3, 8, N), f32),
            vmem((N, 4 * N), bf16),
            vmem((SLOTS, 2, N, N), f32),
            vmem((SLOTS, 4 * N, N), bf16),
            vmem((SLOTS, N, 4 * N), bf16),
            vmem((SLOTS, N, 4 * N), bf16),
            vmem((SLOTS, N, 2 * N), f32),
            vmem((2 * N, N), f32),
            vmem((SLOTS, 2, N, N), f32),
            vmem((SLOTS, 2, N, N), f32),
            vmem((N, 4 * N), bf16),
            vmem((4 * N, N), bf16),
            vmem((2, 2 * TR, TC + N), f32),
            vmem((2, TR, N), f32),
            vmem((2, TR, TC), f32),
            vmem((2, TR, N), f32),
            vmem((2, N, N), f32),
            vmem((N, N), f32),
            vmem((N // (8 * nz), nz, 8, N), f32),
            vmem((nz, N // (8 * nz), 8, N), f32),
            vmem((ny, 8, 128), f32),
            vmem((ny, 8, 128), f32),
            vmem((4, 8, 128), f32),
            vmem((2, N, N), f32),
            dma((8,)), dma((2 + 4 * PARTS,)), dma((2 + 4 * PARTS,)), dma((2,)), dma((2,)),
            dma((2 * ny,)), dma((2 * ny,)), dma((2 * nz,)), dma((2 * nz,)), dma((4,)), dma((4,)),
        ],
        compiler_params=pltpu.CompilerParams(collective_id=0, has_side_effects=True, vmem_limit_bytes=56 * 2**20),
    )(offsets.T, counts, object_field, probe_field, intensity, jnp.asarray(dft_tables()), *(jnp.asarray(t) for t in twiddles()))
    return grad, probe_grad


def solution(mesh):
    in_specs = (
        P(None, "row", "col"),
        P(),
        P(("row", "col"), None, None),
        P(("row", "col"), None),
        P(("row", "col")),
    )
    out_specs = (P(None, "row", "col"), P())
    body = functools.partial(local, mesh.shape["row"], mesh.shape["col"])
    return jax.shard_map(body, mesh=mesh, in_specs=in_specs, out_specs=out_specs, check_vma=False)
```

```python
import functools
import math

import jax
import jax.numpy as jnp
import ml_dtypes
import numpy as np
from jax import lax
from jax.experimental import pallas as pl
from jax.experimental.pallas import tpu as pltpu
from jax.sharding import PartitionSpec as P

MESH = pl.DeviceIdType.MESH
f32 = jnp.float32
bf16 = jnp.bfloat16
stabilizer = 0.01
N = 256
TR = 256
TC = 512
SLOTS = 4
CH = 32
M = N // 2
PARTS = 4


def dft_tables():
    index = np.arange(M)
    angles = (index[:, None] * index[None, :] % M) * (2.0 * np.pi / M)
    c = np.cos(angles) / math.sqrt(N)
    s = np.sin(angles) / math.sqrt(N)
    both = np.stack([np.block([[c, -s], [s, c]]), np.block([[c, s], [-s, c]])]).astype(np.float32)
    high = both.astype(ml_dtypes.bfloat16)
    low = (both - high.astype(np.float32)).astype(ml_dtypes.bfloat16)
    return np.stack([high, low], axis=1)


def twiddles():
    angles = np.arange(M) * (2.0 * np.pi / N)
    pair = np.stack([np.cos(angles), np.sin(angles)]).astype(np.float32)
    return np.broadcast_to(pair[:, :, None], (2, M, N)).copy(), np.broadcast_to(pair[:, None, :], (2, N, M)).copy()


def rows(start, size):
    return pl.ds(pl.multiple_of(start, 8), size)


def split(value):
    high = value.astype(bf16)
    return high, (value - high.astype(f32)).astype(bf16)


def dot(a, b):
    return jnp.dot(a, b, preferred_element_type=f32)


def forward_half(tops, bottoms, cosine, sine):
    real, imag = tops[0] - bottoms[0], tops[1] - bottoms[1]
    odd = (real * cosine + imag * sine, imag * cosine - real * sine)
    return (tops[0] + bottoms[0], tops[1] + bottoms[1]), odd


def backward_half(even, odd, cosine, sine):
    real, imag = odd[0] * cosine - odd[1] * sine, odd[0] * sine + odd[1] * cosine
    return (even[0] + real, even[1] + imag), (even[0] - real, even[1] - imag)


def kernel(
    nrow, ncol,
    offs, cnt, obj, probe_in, inten_in, tab_in, row_turn_in, lane_turn_in,
    grad_out, pg_out,
    ext, probe, inten, tab, row_turn, lane_turn, Ip, Rs, Rt, Cs, Ct, rvec, cvec, lvec, cmask, Pw, Pc, X, Y, Pj, D, B, patch, ex, Tc, Uc, G, kbuf, lbuf, rbuf,
    pgl, crecv, H, zrecv, ysrc, yrecv, xbuf, res,
    local_sem, halo_send, halo_recv, core_send, core_recv, y_send, y_recv, z_send, z_recv, x_send, x_recv,
):
    ny, nz = nrow // 4, ncol // 2
    row, col = lax.axis_index("row"), lax.axis_index("col")
    y, x_lo, core = row // 4, (row // 2) % 2, row % 2
    x_hi, z = col // nz, col % nz
    x = x_hi * 2 + x_lo
    has_up, has_down = row > 0, row < nrow - 1
    has_left, has_right = col > 0, col < ncol - 1
    partner = row + 1 - 2 * core

    def y_peer(k):
        return lax.rem(y + k, ny)

    def z_peer(k):
        return lax.rem(z + k, nz)

    def x_peer(k):
        return lax.rem(x + k, 4)

    def y_id(k):
        return (y_peer(k) * 4 + x_lo * 2 + core, col)

    def z_id(k):
        return (row, x_hi * nz + z_peer(k))

    def x_id(k):
        other = x_peer(k)
        return (y * 4 + lax.rem(other, 2) * 2 + core, (other // 2) * nz + z)

    loads = [
        pltpu.make_async_copy(obj, ext.at[:, pl.ds(0, TR), pl.ds(0, TC)], local_sem.at[0]),
        pltpu.make_async_copy(probe_in, probe, local_sem.at[1]),
        pltpu.make_async_copy(inten_in, inten, local_sem.at[2]),
        pltpu.make_async_copy(tab_in, tab, local_sem.at[3]),
        pltpu.make_async_copy(row_turn_in, row_turn, local_sem.at[6]),
        pltpu.make_async_copy(lane_turn_in, lane_turn, local_sem.at[7]),
    ]
    loads[1].start()

    barrier = pltpu.get_barrier_semaphore()

    def greet(device):
        pl.semaphore_signal(barrier, inc=1, device_id=device, device_id_type=MESH)

    for k in range(1, ny):
        greet(y_id(k))
    for k in range(1, nz):
        greet(z_id(k))
    for k in range(1, 4):
        greet(x_id(k))
    far_right = has_right & (z == nz - 1)
    far_left = has_left & (z == 0)

    @pl.when(has_up)
    def _():
        greet((row - 1, col))

    @pl.when(has_down)
    def _():
        greet((row + 1, col))

    @pl.when(far_left)
    def _():
        greet((row, col - 1))

    @pl.when(far_right)
    def _():
        greet((row, col + 1))

    loads[0].start()
    loads[2].start()
    loads[3].start()
    loads[4].start()
    loads[5].start()
    one = lambda flag: flag.astype(jnp.int32)
    pl.semaphore_wait(barrier, ny + nz + 1 + one(has_up) + one(has_down) + one(far_left) + one(far_right))

    def halo(index, source, target, device):
        return pltpu.make_async_remote_copy(
            src_ref=source, dst_ref=target, send_sem=halo_send.at[index], recv_sem=halo_recv.at[index],
            device_id=device, device_id_type=MESH,
        )

    up_id = (lax.max(row - 1, 0), col)
    down_id = (lax.min(row + 1, nrow - 1), col)
    left_id = (row, lax.max(col - 1, 0))
    right_id = (row, lax.min(col + 1, ncol - 1))
    top, bottom = pl.ds(0, TR), pl.ds(TR, TR)
    main, side = pl.ds(0, TC), pl.ds(TC, N)
    step = TR // PARTS
    strips = [pl.ds(b * step, step) for b in range(PARTS)]
    lower_strips = [pl.ds(TR + b * step, step) for b in range(PARTS)]
    right_in = [
        halo(2 + b, obj.at[:, strips[b], pl.ds(0, N)], ext.at[:, strips[b], side], left_id) for b in range(PARTS)
    ]
    corner_in = [
        halo(2 + PARTS + b, ext.at[:, strips[b], side], ext.at[:, lower_strips[b], side], up_id) for b in range(PARTS)
    ]
    lower_in = halo(0, obj, ext.at[:, bottom, main], up_id)

    @pl.when(has_left)
    def _():
        for copy in right_in:
            copy.start()

    @pl.when(has_up)
    def _():
        lower_in.start()

    @pl.when(jnp.logical_not(has_right))
    def _():
        ext[:, :, TC:] = jnp.zeros((2, 2 * TR, N), f32)

    @pl.when(jnp.logical_not(has_down))
    def _():
        ext[:, TR:, :] = jnp.zeros((2, TR, TC + N), f32)

    @pl.when(jnp.logical_not(has_up))
    def _():
        kbuf[...] = jnp.zeros_like(kbuf)
        lbuf[...] = jnp.zeros_like(lbuf)

    @pl.when(jnp.logical_not(has_left))
    def _():
        rbuf[...] = jnp.zeros_like(rbuf)

    lanes = lax.broadcasted_iota(jnp.int32, (CH, N), 1)
    lines = lax.broadcasted_iota(jnp.int32, (CH, N), 0)

    def one_hot(flag):
        return jnp.where(flag, 1.0, 0.0).astype(bf16)

    for s in range(SLOTS):
        r = jnp.full((CH, N), offs[0, s], jnp.int32) - row * TR
        c = jnp.full((CH, N), offs[1, s], jnp.int32) - col * TC
        rvec[s] = r
        cvec[s] = c
        lvec[s] = jnp.where(jnp.full((CH, N), cnt[0], jnp.int32) > s, 1.0, 0.0)
        for b in range(3):
            cmask[s, b] = jnp.where((lanes + N * b >= c) & (lanes + N * b < c + N), 1.0, 0.0)[:8]

    def permutations(s, _):
        r, c = rvec[s], cvec[s]

        def body(i, _):
            line = lines + i * CH
            Rs[s, rows(i * CH, CH), :] = one_hot(line == ((lanes + r) & (N - 1)))
            Rt[s, rows(i * CH, CH), :] = one_hot(lanes == ((line + r) & (N - 1)))
            Cs[s, rows(i * CH, CH), :] = one_hot(lanes == ((line + c) & (N - 1)))
            Ct[s, rows(i * CH, CH), :] = one_hot(line == ((lanes + c) & (N - 1)))
            return 0

        lax.fori_loop(0, N // CH, body, 0)
        return 0

    lax.fori_loop(0, SLOTS, permutations, 0)

    loads[1].wait()

    def split_probe(i, _):
        here = rows(i * CH, CH)
        for q in range(2):
            high, low = split(probe[q, here, :])
            Pw[here, q * N:(q + 1) * N] = high
            Pw[here, (q + 2) * N:(q + 3) * N] = low
        return 0

    lax.fori_loop(0, N // CH, split_probe, 0)

    def shift_probe(s, _):
        a = dot(Rs[s], Pw[...])
        for p in range(4):
            Uc[p * N:(p + 1) * N, :] = a[:, p * N:(p + 1) * N].astype(bf16)
        a = dot(Uc[...], Cs[s])
        for q in range(2):
            Pc[s, q] = a[q * N:(q + 1) * N] + a[(q + 2) * N:(q + 3) * N]
        return 0

    lax.fori_loop(0, SLOTS, shift_probe, 0)

    loads[2].wait()
    line, lane = lax.broadcasted_iota(jnp.int32, (N, N), 0), lax.broadcasted_iota(jnp.int32, (N, N), 1)
    sort_rows = one_hot(lane == jnp.where(line < M, 2 * line, 2 * line - (N - 1)))
    sort_lanes = one_hot(line == jnp.where(lane < M, 2 * lane, 2 * lane - (N - 1)))

    def sort_intensity(s, _):
        high, low = split(inten[s])
        Uc[:N, :] = dot(sort_rows, high).astype(bf16)
        Uc[N:2 * N, :] = dot(sort_rows, low).astype(bf16)
        a = dot(Uc[:2 * N, :], sort_lanes)
        a = a[:N] + a[N:]
        Ip[s, :, :N] = a[:M]
        Ip[s, :, N:] = a[M:]
        return 0

    lax.fori_loop(0, SLOTS, sort_intensity, 0)

    @pl.when(has_right)
    def _():
        for b in range(PARTS):
            right_in[b].wait_recv()

            @pl.when(has_up)
            def _():
                corner_in[b].start()

    for load in (loads[0], loads[3], loads[4], loads[5]):
        load.wait()

    @pl.when(has_down)
    def _():
        lower_in.wait_recv()

        @pl.when(has_right)
        def _():
            for copy in corner_in:
                copy.wait_recv()

    def slot(s, _):
        def gather(i, _):
            i0 = i * CH
            from_below = lines + i0 < rvec[s]
            first, second = lanes >= cvec[s], lanes + N >= cvec[s]
            parts = []
            for q in range(2):
                u = ext[q, rows(i0, CH), :]
                v = ext[q, rows(i0 + TR, CH), :]
                blocks = [jnp.where(from_below, v[:, b * N:(b + 1) * N], u[:, b * N:(b + 1) * N]) for b in range(3)]
                w = jnp.where(first, blocks[0], jnp.where(second, blocks[1], blocks[2]))
                patch[s, q, rows(i0, CH), :] = w
                parts.append(w)
            pr, pi = Pc[s, 0, rows(i0, CH), :], Pc[s, 1, rows(i0, CH), :]
            waves = (pr * parts[0] - pi * parts[1], pr * parts[1] + pi * parts[0])
            for q, wave in enumerate(waves):
                ex[s, q, rows(i0, CH), :] = wave
            turn = (lane_turn[0, rows(i0, CH), :], lane_turn[1, rows(i0, CH), :])
            pair = forward_half([w[:, :M] for w in waves], [w[:, M:] for w in waves], *turn)
            for b in range(2):
                for q in range(2):
                    high, low = split(pair[b][q])
                    X[s, rows(i0 + b * N, CH), q * M:(q + 1) * M] = high
                    X[s, rows(i0 + (b + 2) * N, CH), q * M:(q + 1) * M] = low
            return 0

        lax.fori_loop(0, N // CH, gather, 0, unroll=8)
        a = dot(X[s], tab[0, 0])
        a = a[:2 * N] + a[2 * N:] + dot(X[s, :2 * N], tab[0, 1])
        a = [jnp.concatenate([a[:N, q * M:(q + 1) * M], a[N:, q * M:(q + 1) * M]], axis=1) for q in range(2)]
        pair = forward_half([w[:M] for w in a], [w[M:] for w in a], row_turn[0], row_turn[1])
        for b in range(2):
            for q in range(2):
                high, low = split(pair[b][q])
                Y[s, q * M:(q + 1) * M, b * N:(b + 1) * N] = high
                Y[s, q * M:(q + 1) * M, (b + 2) * N:(b + 3) * N] = low
        a = dot(tab[1, 0], Y[s])
        D[s] = a[:, :2 * N] + a[:, 2 * N:] + dot(tab[1, 1], Y[s, :, :2 * N])

        def project(i, _):
            i0 = i * 16
            zr, zi = D[s, rows(i0, 16), :], D[s, rows(i0 + M, 16), :]
            measured = Ip[s, rows(i0, 16), :]
            factor = measured * lax.rsqrt(measured * (zr * zr + zi * zi + stabilizer))
            for q, wave in enumerate((zr * factor, zi * factor)):
                high, low = split(wave)
                there = pl.ds(pl.multiple_of(i0 + q * M, 16), 16)
                Pj[s, there, :2 * N] = high
                Pj[s, there, 2 * N:] = low
            return 0

        lax.fori_loop(0, M // 16, project, 0, unroll=8)
        a = dot(tab[0, 0], Pj[s])
        a = a[:, :2 * N] + a[:, 2 * N:] + dot(tab[0, 1], Pj[s, :, :2 * N])
        pair = backward_half((a[:M, :N], a[M:, :N]), (a[:M, N:], a[M:, N:]), row_turn[0], row_turn[1])
        for b in range(2):
            for q in range(2):
                high, low = split(pair[b][q])
                for part in range(2):
                    there = slice(part * N + b * M, part * N + (b + 1) * M)
                    below = slice((part + 2) * N + b * M, (part + 2) * N + (b + 1) * M)
                    X[s, there, q * M:(q + 1) * M] = high[:, part * M:(part + 1) * M]
                    X[s, below, q * M:(q + 1) * M] = low[:, part * M:(part + 1) * M]
        a = dot(X[s], tab[1, 0])
        a = a[:2 * N] + a[2 * N:] + dot(X[s, :2 * N], tab[1, 1])
        pair = backward_half((a[:N, :M], a[:N, M:]), (a[N:, :M], a[N:, M:]), lane_turn[0], lane_turn[1])
        for b in range(2):
            for q in range(2):
                B[q * N:(q + 1) * N, b * M:(b + 1) * M] = pair[b][q]

        def finish(i, _):
            i0 = i * CH
            here, below = rows(i0, CH), rows(i0 + N, CH)
            live = lvec[s]
            dr = (ex[s, 0, here, :] - B[here, :]) * live
            di = (ex[s, 1, here, :] - B[below, :]) * live
            wr, wi = patch[s, 0, here, :], patch[s, 1, here, :]
            for q, term in enumerate((wr * dr + wi * di, wr * di - wi * dr)):
                high, low = split(term)
                Tc[here, q * N:(q + 1) * N] = high
                Tc[here, (q + 2) * N:(q + 3) * N] = low
            pr, pi = Pc[s, 0, here, :], Pc[s, 1, here, :]
            ex[s, 0, here, :] = pr * dr + pi * di
            ex[s, 1, here, :] = pr * di - pi * dr
            return 0

        lax.fori_loop(0, N // CH, finish, 0, unroll=8)

        a = dot(Rt[s], Tc[...])
        for q in range(2):
            high, low = split(a[:, q * N:(q + 1) * N] + a[:, (q + 2) * N:(q + 3) * N])
            Uc[q * N:(q + 1) * N, :] = high
            Uc[(q + 2) * N:(q + 3) * N, :] = low
        a = dot(Uc[...], Ct[s])
        for q in range(2):
            pgl[q] += a[q * N:(q + 1) * N] + a[(q + 2) * N:(q + 3) * N]
        return 0

    pgl[...] = jnp.zeros_like(pgl)
    lax.fori_loop(0, SLOTS, slot, 0, unroll=2)

    def remote(source, target, send, recv, device):
        return pltpu.make_async_remote_copy(
            src_ref=source, dst_ref=target, send_sem=send, recv_sem=recv, device_id=device, device_id_type=MESH
        )

    to_partner = remote(pgl.at[1 - core], crecv, core_send.at[0], core_recv.at[0], (partner, col))
    to_partner.start()

    def deposit(i, _):
        i0 = i * 8
        here, below = rows(i0, 8), rows(i0 + N, 8)
        for q in range(2):
            terms = [ex[s, q, here, :] for s in range(SLOTS)]
            lower = [jnp.where(lines[:8] + i0 < rvec[s, :8], terms[s], 0.0) for s in range(SLOTS)]
            upper = [terms[s] - lower[s] for s in range(SLOTS)]
            for b in range(3):
                for part, target in ((lower, below), (upper, here)):
                    kept = [part[s] * cmask[s, b] for s in range(SLOTS)]
                    G[q, target, b * N:(b + 1) * N] = (kept[0] + kept[1]) + (kept[2] + kept[3])
        return 0

    lax.fori_loop(0, N // 8, deposit, 0, unroll=4)

    corner_out = [
        halo(2 + 2 * PARTS + b, G.at[:, lower_strips[b], side], kbuf.at[:, strips[b], :], down_id) for b in range(PARTS)
    ]
    right_out = [
        halo(2 + 3 * PARTS + b, G.at[:, strips[b], side], rbuf.at[:, strips[b], :], right_id) for b in range(PARTS)
    ]
    lower_out = halo(1, G.at[:, bottom, main], lbuf, down_id)

    @pl.when(has_down)
    def _():
        for copy in corner_out:
            copy.start()
        lower_out.start()

    to_partner.wait_recv()

    def add_core(i, _):
        for p in range(nz):
            here = rows(i * nz * 8 + p * 8, 8)
            H[i, p] = pgl[core, here, :] + crecv[here, :]
        return 0

    lax.fori_loop(0, N // (8 * nz), add_core, 0, unroll=True)
    z_out = [remote(H.at[:, z_peer(k)], zrecv.at[k], z_send.at[k], z_recv.at[k], z_id(k)) for k in range(1, nz)]
    for copy in z_out:
        copy.start()

    for copy in z_out:
        copy.wait_recv()
    for a in range(N // (8 * nz)):
        summed = H[a, z]
        for k in range(1, nz):
            summed = summed + zrecv[k, a]
        for half in range(2):
            ysrc[2 * a + half] = summed[:, 128 * half:128 * half + 128]
    y_out = [remote(ysrc.at[y_peer(k)], yrecv.at[k], y_send.at[k], y_recv.at[k], y_id(k)) for k in range(1, ny)]
    for copy in y_out:
        copy.start()
    def add_corner(i, _):
        for q in range(2):
            G[q, rows(i * CH, CH), TC:] += kbuf[q, rows(i * CH, CH), :]
        return 0

    def pass_corner(b):
        @pl.when(has_up)
        def _():
            corner_out[b].wait_recv()

        lax.fori_loop(b * step // CH, (b + 1) * step // CH, add_corner, 0, unroll=True)

        @pl.when(has_right)
        def _():
            right_out[b].start()

    for b in range(PARTS):
        pass_corner(b)

    for copy in y_out:
        copy.wait_recv()
    tile = ysrc[y]
    for k in range(1, ny):
        tile = tile + yrecv[k]
    xbuf[x] = tile
    x_out = [remote(xbuf.at[x], xbuf.at[x], x_send.at[k], x_recv.at[k], x_id(k)) for k in range(1, 4)]
    for copy in x_out:
        copy.start()
    for copy in x_out:
        copy.wait_recv()
    tile = ((xbuf[0] + xbuf[1]) + (xbuf[2] + xbuf[3])) * f32(1.0 / math.sqrt(SLOTS * nrow * ncol))
    my_lanes = pl.ds(pl.multiple_of(128 * (y % 2), 128), 128)
    my_tile = (core, rows(8 * nz * (y // 2) + 8 * z, 8), my_lanes)
    res[my_tile] = tile
    z_back = [remote(res.at[my_tile], res.at[my_tile], z_send.at[nz + k], z_recv.at[nz + k], z_id(k)) for k in range(1, nz)]
    for copy in z_back:
        copy.start()

    for copy in z_back:
        copy.wait_recv()
    my_rows = (core, rows(8 * nz * (y // 2), 8 * nz), my_lanes)
    y_back = [remote(res.at[my_rows], res.at[my_rows], y_send.at[ny + k], y_recv.at[ny + k], y_id(k)) for k in range(1, ny)]
    for copy in y_back:
        copy.start()
    shares = []
    for k in range(ny):
        if k > 0:
            y_back[k - 1].wait_recv()
        owner = lax.rem(y - k + ny, ny)
        piece = res.at[core, rows(8 * nz * (owner // 2), 8 * nz), pl.ds(pl.multiple_of(128 * (owner % 2), 128), 128)]
        shares.append(remote(piece, piece, core_send.at[1 + k], core_recv.at[1 + k], (partner, col)))
        shares[k].start()

    @pl.when(has_up)
    def _():
        lower_out.wait_recv()

    @pl.when(has_left)
    def _():
        for copy in right_out:
            copy.wait_recv()

    def add_halos(i, _):
        here = rows(i * CH, CH)
        for q in range(2):
            G[q, here, :N] = G[q, here, :N] + lbuf[q, here, :N] + rbuf[q, here, :]
            G[q, here, N:TC] = G[q, here, N:TC] + lbuf[q, here, N:]
        return 0

    lax.fori_loop(0, TR // CH, add_halos, 0, unroll=8)
    store_grad = pltpu.make_async_copy(G.at[:, top, main], grad_out, local_sem.at[4])
    store_grad.start()
    for copy in shares:
        copy.wait_recv()
    store_probe = pltpu.make_async_copy(res, pg_out, local_sem.at[5])
    store_probe.start()

    @pl.when(has_left)
    def _():
        for copy in right_in:
            copy.wait_send()

    @pl.when(has_up)
    def _():
        lower_in.wait_send()

        @pl.when(has_right)
        def _():
            for copy in corner_in:
                copy.wait_send()

    @pl.when(has_down)
    def _():
        for copy in corner_out:
            copy.wait_send()
        lower_out.wait_send()

    @pl.when(has_right)
    def _():
        for copy in right_out:
            copy.wait_send()

    to_partner.wait_send()
    for copy in shares:
        copy.wait_send()
    for copy in y_out + z_out + x_out + z_back + y_back:
        copy.wait_send()
    store_grad.wait()
    store_probe.wait()


def local(nrow, ncol, object_field, probe_field, intensity, offsets, counts):
    ny, nz = nrow // 4, ncol // 2
    anywhere = pl.BlockSpec(memory_space=pl.ANY)
    scalars = pl.BlockSpec(memory_space=pltpu.SMEM)
    vmem = pltpu.VMEM
    dma = pltpu.SemaphoreType.DMA
    grad, probe_grad = pl.pallas_call(
        functools.partial(kernel, nrow, ncol),
        out_shape=[jax.ShapeDtypeStruct((2, TR, TC), f32), jax.ShapeDtypeStruct((2, N, N), f32)],
        in_specs=[scalars, scalars] + [anywhere] * 6,
        out_specs=[anywhere, anywhere],
        scratch_shapes=[
            vmem((2, 2 * TR, TC + N), f32),
            vmem((2, N, N), f32),
            vmem((SLOTS, N, N), f32),
            vmem((2, 2, N, N), bf16),
            vmem((2, M, N), f32),
            vmem((2, N, M), f32),
            vmem((SLOTS, M, 2 * N), f32),
            vmem((SLOTS, N, N), bf16),
            vmem((SLOTS, N, N), bf16),
            vmem((SLOTS, N, N), bf16),
            vmem((SLOTS, N, N), bf16),
            vmem((SLOTS, CH, N), jnp.int32),
            vmem((SLOTS, CH, N), jnp.int32),
            vmem((SLOTS, CH, N), f32),
            vmem((SLOTS, 3, 8, N), f32),
            vmem((N, 4 * N), bf16),
            vmem((SLOTS, 2, N, N), f32),
            vmem((SLOTS, 4 * N, N), bf16),
            vmem((SLOTS, N, 4 * N), bf16),
            vmem((SLOTS, N, 4 * N), bf16),
            vmem((SLOTS, N, 2 * N), f32),
            vmem((2 * N, N), f32),
            vmem((SLOTS, 2, N, N), f32),
            vmem((SLOTS, 2, N, N), f32),
            vmem((N, 4 * N), bf16),
            vmem((4 * N, N), bf16),
            vmem((2, 2 * TR, TC + N), f32),
            vmem((2, TR, N), f32),
            vmem((2, TR, TC), f32),
            vmem((2, TR, N), f32),
            vmem((2, N, N), f32),
            vmem((N, N), f32),
            vmem((N // (8 * nz), nz, 8, N), f32),
            vmem((nz, N // (8 * nz), 8, N), f32),
            vmem((ny, 8, 128), f32),
            vmem((ny, 8, 128), f32),
            vmem((4, 8, 128), f32),
            vmem((2, N, N), f32),
            dma((8,)), dma((2 + 4 * PARTS,)), dma((2 + 4 * PARTS,)), dma((9,)), dma((9,)),
            dma((2 * ny,)), dma((2 * ny,)), dma((2 * nz,)), dma((2 * nz,)), dma((4,)), dma((4,)),
        ],
        compiler_params=pltpu.CompilerParams(collective_id=0, has_side_effects=True, vmem_limit_bytes=56 * 2**20),
    )(offsets.T, counts, object_field, probe_field, intensity, jnp.asarray(dft_tables()), *(jnp.asarray(t) for t in twiddles()))
    return grad, probe_grad


def solution(mesh):
    in_specs = (
        P(None, "row", "col"),
        P(),
        P(("row", "col"), None, None),
        P(("row", "col"), None),
        P(("row", "col")),
    )
    out_specs = (P(None, "row", "col"), P())
    body = functools.partial(local, mesh.shape["row"], mesh.shape["col"])
    return jax.shard_map(body, mesh=mesh, in_specs=in_specs, out_specs=out_specs, check_vma=False)
```
